32 devices in a mesh: texel: 2 (over x), light: 4 (over z), view: 4 (over y, core).
Axes of the slice: x: 2, y: 2, z: 4, core: 2. Of those that a mesh axis runs over, the one named last changes fastest.
Arguments:
- slab: bfloat16 [80, 80, 2048], P('light', 'view', 'texel'), may hold values from -6 to 6
- basis: bfloat16 [80, 48], P('view'), may hold values from -0.625 to 0.625
Outputs:
- view_gram: float32 [80, 80], P('view')
- core: bfloat16 [48, 80, 2048], P('view', 'light', 'texel')
- light_gram: float32 [80, 80], P('light')
The draws below stay inside these ranges and needn't reach their ends.
All inputs are finite; a program needn't handle non-finite values.
Results may differ from the reference program's by a relative error of at most 0.001.
Values may be sent and summed in bfloat16 or wider, within the bound.
No kernel may reach another device: no remote copies, remote signals or barrier semaphores. Data moves between devices by JAX's collectives and lax.ppermute only.
A program may use at most 64 MiB of HBM per device.

```python
import jax
import jax.numpy as jnp
from jax import lax

LIGHTS = 80
VIEWS = 80
RANK = 48
COLUMNS = 2048


def block_levels(stream_key, shape, pieces, smallest, top_value):
    level, own = 1.0, jax.random.fold_in(stream_key, 6)
    for position, shards_of in pieces:
        heights = jnp.exp(jax.random.uniform(jax.random.fold_in(own, position), (shards_of,), jnp.float32, smallest / len(pieces), top_value / len(pieces)))
        level = level * jnp.repeat(heights, shape[position] // shards_of).reshape([-1 if axis == position else 1 for axis in range(len(shape))])
    return level


def noise(key, extent, width, bound, split=(), kind=jnp.bfloat16):
    entries = width * jax.random.normal(key, extent, jnp.float32)
    if split:
        entries = entries * block_levels(key, extent, split, -0.22, 0.18)
    return jnp.clip(entries, -bound, bound).astype(kind)


def setup_inputs(seed: int = 0) -> dict:
    key_of = jax.random.split(jax.random.key(seed), 3)
    slab = noise(key_of[0], (LIGHTS, VIEWS, COLUMNS), 1.0, 6.0, ((0, 4), (1, 4), (2, 2)))
    basis = noise(key_of[1], (VIEWS, RANK), VIEWS ** -0.5, 0.625, ((0, 4),))
    return dict(slab=slab, basis=basis)


def reference(slab, basis):
    def view_part(total, page):
        return total + jnp.dot(page, page.T, preferred_element_type=jnp.float32), None

    view_gram, unused = lax.scan(view_part, jnp.zeros((VIEWS, VIEWS), jnp.float32), slab)
    view_gram = view_gram / (LIGHTS * COLUMNS)
    basis_turned = basis.T

    def truncate(page):
        return jnp.dot(basis_turned, page, preferred_element_type=jnp.float32).astype(jnp.bfloat16)

    core_lights = lax.map(truncate, slab)
    flat = core_lights.reshape(LIGHTS, RANK * COLUMNS)
    light_gram = lax.dot_general(flat, flat, (((1,), (1,)), ((), ())), preferred_element_type=jnp.float32)
    light_gram = light_gram / (RANK * COLUMNS)
    return view_gram, jnp.transpose(core_lights, (1, 0, 2)), light_gram
```

```python
import functools

import jax
import jax.numpy as jnp
from jax import lax
from jax.experimental import pallas as pl
from jax.experimental.pallas import tpu as pltpu
from jax.sharding import PartitionSpec as P

VMEM = pl.BlockSpec(memory_space=pltpu.VMEM)
PARAMS = pltpu.CompilerParams(vmem_limit_bytes=32 * 1024 * 1024)
sds = jax.ShapeDtypeStruct


def swap(value, axis, step):
    return lax.ppermute(value, axis, [(i, i ^ step) for i in range(lax.axis_size(axis))])


def swaps(values, axis):
    moved = {k: swap(values[k], axis, k) for k in range(len(values) - 1, 0, -1)}
    return [values[0]] + [moved[k] for k in range(1, len(values))]


def doubled(value, axis):
    step = 1
    while step < lax.axis_size(axis):
        value = value + swap(value, axis, step)
        step *= 2
    return value


def call(kernel, out_shape, scratch, flops, *args):
    moved = sum(a.size * a.dtype.itemsize for a in list(args) + jax.tree.leaves(out_shape))
    return pl.pallas_call(
        kernel,
        out_shape=out_shape,
        in_specs=[VMEM] * len(args),
        out_specs=jax.tree.map(lambda _: VMEM, out_shape),
        scratch_shapes=scratch,
        compiler_params=PARAMS,
        cost_estimate=pl.CostEstimate(flops=flops, bytes_accessed=moved, transcendentals=0),
    )(*args)


def nt(a, b):
    return lax.dot_general(a, b, (((1,), (1,)), ((), ())), preferred_element_type=jnp.float32)


def pack_kernel(slab_ref, basis_ref, *outs):
    me = lax.axis_index("view")
    lights, rows, columns = slab_ref.shape
    ranks = basis_ref.shape[1]
    width = columns // len(outs)
    rest = outs[0].shape[0] - (lights + 1) * rows
    basis = jnp.pad(basis_ref[...], ((0, rest), (0, width - ranks)))
    for k in range(len(outs)):
        at = pl.ds(pl.multiple_of((me ^ k) * width, width), width)
        outs[k][...] = jnp.concatenate([slab_ref[l, :, at] for l in range(lights)] + [basis], axis=0)


def core_kernel(lights, rows, ranks, views, parts, scale, *refs):
    ins, refs = refs[:views], refs[views:]
    light_outs, refs = refs[:parts], refs[parts:]
    view_outs, refs = refs[:views], refs[views:]
    gram_outs, refs = refs[:views], refs[views:]
    whole, turned, pieces, grams = refs
    v, z = lax.axis_index("view"), lax.axis_index("light")
    width = whole.shape[2]
    for k in range(views):
        whole[v ^ k] = ins[k][...]
    body = lights * rows
    basis = jnp.concatenate([whole[k, body : body + rows, :128] for k in range(views)], axis=0)
    basis = basis.astype(jnp.float32).T[:ranks].astype(jnp.bfloat16)
    gram = jnp.zeros((views * rows, views * rows), jnp.float32)
    for l in range(lights):
        page = jnp.concatenate([whole[k, l * rows : (l + 1) * rows, :] for k in range(views)], axis=0)
        product = jnp.dot(basis, page, preferred_element_type=jnp.float32)
        for h in range(width // 128):
            turned[h, l * ranks : (l + 1) * ranks, :] = product[:, h * 128 : (h + 1) * 128]
        gram += nt(page, page)
    gram *= scale
    size = ranks // parts
    for j in range(parts):
        for h in range(width // 128):
            picked = [turned[h, pl.ds(j * size + r, lights, stride=ranks), :] for r in range(size)]
            pieces[j, :, h * 128 : (h + 1) * 128] = jnp.concatenate(picked, axis=0).astype(jnp.bfloat16)
    for k in range(parts):
        light_outs[k][...] = pieces[z ^ k]
    for k in range(views):
        grams[k] = gram[k * rows : (k + 1) * rows]
    for k in range(views):
        view_outs[k][...] = pieces[v ^ k]
        gram_outs[k][...] = grams[v ^ k]


def light_kernel(lights, parts, scale, *refs):
    ins, refs = refs[:parts], refs[parts:]
    extra, outs, whole, grams = refs[0], refs[1 : parts + 1], refs[-2], refs[-1]
    z = lax.axis_index("light")
    for k in range(parts):
        whole[z ^ k] = ins[k][...]
    gram = jnp.zeros((parts * lights, parts * lights), jnp.float32)
    for r in range(whole.shape[1] // lights):
        page = jnp.concatenate([whole[k, r * lights : (r + 1) * lights, :] for k in range(parts)], axis=0)
        gram += nt(page, page)
    gram *= scale
    for k in range(parts):
        grams[k] = gram[k * lights : (k + 1) * lights]
    for k in range(parts):
        outs[k][...] = jnp.concatenate([grams[z ^ k], extra[...]], axis=0)


def place_kernel(lights, *refs):
    ins, core_ref = refs[:-1], refs[-1]
    v = lax.axis_index("view")
    width = ins[0].shape[1]
    for k in range(len(ins)):
        at = pl.ds(pl.multiple_of((v ^ k) * width, width), width)
        for r in range(core_ref.shape[0]):
            core_ref[r, :, at] = ins[k][r * lights : (r + 1) * lights, :]


def body(slab, basis):
    views, parts = lax.axis_size("view"), lax.axis_size("light")
    lights, rows, columns = slab.shape
    ranks = basis.shape[1]
    columns_all = columns * lax.axis_size("texel")
    view_scale = 1.0 / (lights * parts * columns_all)
    light_scale = 1.0 / (ranks * columns_all)
    width = columns // views
    packed_rows = -(-(lights + 1) * rows // 16) * 16
    views_all, lights_all = views * rows, parts * lights
    piece = ranks // parts * lights
    bf16, f32 = jnp.bfloat16, jnp.float32

    packed = call(pack_kernel, [sds((packed_rows, width), bf16)] * views, [], 0, slab, basis)
    whole = swaps(packed, "view")
    made = call(
        functools.partial(core_kernel, lights, rows, ranks, views, parts, view_scale),
        [sds((piece, width), bf16)] * (parts + views) + [sds((rows, views_all), f32)] * views,
        [
            pltpu.VMEM((views, packed_rows, width), bf16),
            pltpu.VMEM((width // 128, lights * ranks, 128), f32),
            pltpu.VMEM((parts, piece, width), bf16),
            pltpu.VMEM((views, rows, views_all), f32),
        ],
        2 * views_all * lights * width * (views_all + ranks),
        *whole,
    )
    lit = swaps(made[:parts], "light")
    view_gram = sum(swaps(made[parts + views :], "view"))
    view_gram = doubled(view_gram, "texel")
    core_parts = swaps(made[parts : parts + views], "view")
    sums = call(
        functools.partial(light_kernel, lights, parts, light_scale),
        [sds((lights + rows, lights_all), f32)] * parts,
        [pltpu.VMEM((parts, piece, width), bf16), pltpu.VMEM((parts, lights, lights_all), f32)],
        2 * lights_all * lights_all * ranks // parts * width,
        *lit,
        view_gram,
    )
    total = sum(swaps(sums, "light"))
    view_gram = total[lights:]
    light_gram = sum(swaps([total[:lights]] * views, "view"))
    light_gram = doubled(light_gram, "texel")
    core = call(
        functools.partial(place_kernel, lights), sds((ranks // views, lights, columns), bf16), [], 0, *core_parts
    )
    return (view_gram, core, light_gram)


def solution(mesh):
    return jax.shard_map(
        body,
        mesh=mesh,
        in_specs=(P("light", "view", "texel"), P("view", None)),
        out_specs=(P("view", None), P("view", "light", "texel"), P("light", None)),
        check_vma=False,
    )
```

```python
import functools

import jax
import jax.numpy as jnp
from jax import lax
from jax.experimental import pallas as pl
from jax.experimental.pallas import tpu as pltpu
from jax.sharding import PartitionSpec as P

VMEM = pl.BlockSpec(memory_space=pltpu.VMEM)
ANY = pl.BlockSpec(memory_space=pl.ANY)
sds = jax.ShapeDtypeStruct
bf16, f32 = jnp.bfloat16, jnp.float32


def swap(value, axis, step):
    return lax.ppermute(value, axis, [(i, i ^ step) for i in range(lax.axis_size(axis))])


def farthest_first(n):
    return list(range(n - 1, -1, -1))


def swaps(values, axis):
    moved = {k: swap(values[k], axis, k) for k in farthest_first(len(values))[:-1]}
    return [values[0]] + [moved[k] for k in range(1, len(values))]


def summed(values):
    total = values[-1]
    for value in values[-2::-1]:
        total = total + value
    return total


def doubled(value, axis):
    step = 1
    while step < lax.axis_size(axis):
        value = value + swap(value, axis, step)
        step *= 2
    return value


def call(kernel, out_shape, scratch, flops, args, unused=()):
    moved = sum(a.size * a.dtype.itemsize for a in list(args) + jax.tree.leaves(out_shape))
    return pl.pallas_call(
        kernel,
        out_shape=out_shape,
        in_specs=[VMEM] * len(args) + [ANY] * len(unused),
        out_specs=jax.tree.map(lambda _: VMEM, out_shape),
        scratch_shapes=scratch,
        compiler_params=pltpu.CompilerParams(vmem_limit_bytes=32 * 1024 * 1024),
        cost_estimate=pl.CostEstimate(flops=flops, bytes_accessed=moved, transcendentals=0),
    )(*args, *unused)


def nt(a, b):
    return lax.dot_general(a, b, (((1,), (1,)), ((), ())), preferred_element_type=f32)


def cut(refs, *counts):
    out, at = [], 0
    for count in counts:
        out.append(refs[at : at + count])
        at += count
    return out + [refs[at:]]


def blank_kernel(out_ref):
    out_ref[...] = jnp.zeros_like(out_ref)


def pack_kernel(spans, groups, ranks, views, slab_ref, *refs):
    me = lax.axis_index("view")
    outs = refs[-len(spans) :]
    rows, columns = slab_ref.shape[1:]
    width = columns // views
    head = []
    if groups:
        deep = rows // groups
        wide = refs[0][...].astype(f32)
        wide = jnp.concatenate([wide[g * deep : (g + 1) * deep] for g in range(groups)], axis=1)
        head = [jnp.pad(wide, ((0, -deep % 8), (0, width - groups * ranks))).astype(bf16)]
    for (k, begin, count), out in zip(spans, outs):
        at = pl.ds(pl.multiple_of((me ^ k) * width, width), width)
        out[...] = jnp.concatenate(head + [slab_ref[l, :, at] for l in range(begin, begin + count)], axis=0)


def core_kernel(lights, head, starts, rows, ranks, views, parts, groups, spare, *refs):
    first = groups > 0
    ins, old, _, light_outs, (pieces, *outs) = cut(refs[:-2], views, 0 if first else 1, spare, parts)
    whole, turned = refs[-2:]
    v, z = lax.axis_index("view"), lax.axis_index("light")
    width = whole.shape[2]
    for i, k in enumerate(farthest_first(views)):
        whole[v ^ k] = ins[i][starts[i] : starts[i] + whole.shape[1], :]
    if first:
        deep = rows // groups
        wide = [whole[k, :head, :].astype(f32)[:deep] for k in range(views)]
        basis = jnp.concatenate([w[:, g * ranks : (g + 1) * ranks] for w in wide for g in range(groups)], axis=0)
        basis = jnp.pad(basis, ((0, 0), (0, 128 - ranks))).T[:ranks].astype(bf16)
    else:
        basis = old[0][...]
    for l in range(lights):
        at = head + l * rows
        page = jnp.concatenate([whole[k, at : at + rows, :] for k in range(views)], axis=0)
        product = jnp.dot(basis, page, preferred_element_type=f32)
        for h in range(width // 128):
            turned[h, l * ranks : (l + 1) * ranks, :] = product[:, h * 128 : (h + 1) * 128]
    size = ranks // parts
    for j in range(parts):
        for h in range(width // 128):
            picked = [turned[h, pl.ds(j * size + r, lights, stride=ranks), :] for r in range(size)]
            pieces[j, :, h * 128 : (h + 1) * 128] = jnp.concatenate(picked, axis=0).astype(bf16)
    for k in range(parts):
        light_outs[k][...] = pieces[z ^ k]
    if first:
        outs[0][...] = basis


def back_kernel(chunks, *refs):
    v, outs = lax.axis_index("view"), refs[-refs[0].shape[0] :]
    for k, out in enumerate(outs):
        out[...] = jnp.concatenate([ref[v ^ k] for ref in refs[:chunks]], axis=0)


def view_kernel(lights, rows, views, spans, scale, *refs):
    ins, (out, whole) = cut(refs, len(spans))
    v = lax.axis_index("view")
    for (k, begin), ref in zip(spans, ins):
        whole[v ^ k, begin : begin + ref.shape[0], :] = ref[...]
    head = whole.shape[1] - lights * rows
    gram = jnp.zeros((views * rows, views * rows), f32)
    for l in range(lights):
        at = head + l * rows
        page = jnp.concatenate([whole[k, at : at + rows, :] for k in range(views)], axis=0)
        gram += nt(page, page)
    gram *= scale
    half = views * rows // 2
    quarters = jnp.concatenate([gram[:half], gram[half:, half:]], axis=1)
    out[...] = jnp.pad(quarters, ((0, 0), (0, out.shape[1] - 3 * half)))


def deal_kernel(lights, rows, views, *refs):
    ins, outs, (blocks,) = cut(refs, len(refs) - views - 1, views)
    v = lax.axis_index("view")
    total = summed([ref[...] for ref in ins])
    light, quarters = total[:lights, : outs[0].shape[1]], total[lights:]
    half = views * rows // 2
    cross = quarters[:, half : 2 * half]
    lower = jnp.concatenate([cross.T, quarters[:, 2 * half : 3 * half]], axis=1)
    gram = jnp.concatenate([quarters[:, : 2 * half], lower], axis=0)
    for k in range(views):
        blocks[k] = gram[k * rows : (k + 1) * rows]
    for k in range(views):
        outs[k][...] = jnp.concatenate([light, blocks[v ^ k]], axis=0)


def sum_kernel(*refs):
    refs[-1][...] = summed([ref[...] for ref in refs[:-1]])


def light_kernel(counts, spare, parts, scale, *refs):
    ins, (view,), _, outs, wholes, (blocks,) = cut(refs, parts * len(counts), 1, spare, parts, len(counts))
    z, lights = lax.axis_index("light"), sum(counts)
    for c, whole in enumerate(wholes):
        for i, k in enumerate(farthest_first(parts)):
            whole[z ^ k] = ins[c * parts + i][...]
    gram = jnp.zeros((parts * lights, parts * lights), f32)
    for r in range(wholes[0].shape[1] // counts[0]):
        page = [wholes[c][k, r * n : (r + 1) * n, :] for k in range(parts) for c, n in enumerate(counts)]
        page = jnp.concatenate(page, axis=0)
        gram += nt(page, page)
    gram *= scale
    for k in range(parts):
        blocks[k] = gram[k * lights : (k + 1) * lights]
    for k in range(parts):
        block = jnp.pad(blocks[z ^ k], ((0, 0), (0, view.shape[1] - parts * lights)))
        outs[k][...] = jnp.concatenate([block, view[...]], axis=0)


def place_kernel(counts, *refs):
    ins, core_ref = refs[:-1], refs[-1]
    v = lax.axis_index("view")
    ranks, width = core_ref.shape[0], ins[0].shape[1]
    for k in range(len(ins)):
        at = pl.ds(pl.multiple_of((v ^ k) * width, width), width)
        for r in range(ranks):
            begin, page = 0, []
            for n in counts:
                page.append(ins[k][begin + r * n : begin + (r + 1) * n, :])
                begin += ranks * n
            core_ref[r, :, at] = jnp.concatenate(page, axis=0)


def body(slab, basis):
    views, parts = lax.axis_size("view"), lax.axis_size("light")
    lights, rows, columns = slab.shape
    ranks = basis.shape[1]
    columns_all = columns * lax.axis_size("texel")
    view_scale = 1.0 / (lights * parts * columns_all)
    light_scale = 1.0 / (ranks * columns_all)
    width = columns // views
    views_all, lights_all = views * rows, parts * lights
    size = ranks // parts
    groups = max(g for g in range(1, width // ranks + 1) if rows % g == 0)
    head = -(-(rows // groups) // 8) * 8

    one = lights * 2 // 5 // 4 * 4
    counts, half = [one, lights - one], views // 2
    tall = [head + one * rows, (lights - one) * rows]

    blank = call(blank_kernel, sds((8, 128), f32), [], 10**9, [])

    spans = [(k, 0, lights if k < half else one) for k in range(views)]
    packed = call(
        functools.partial(pack_kernel, spans, groups, ranks, views),
        [sds((head + count * rows, width), bf16) for _, _, count in spans],
        [],
        0,
        [slab, basis],
        [blank],
    )
    came = swaps(packed, "view")
    near, whole = came[:half], [came[half:]]
    spans = [(k, one, lights - one) for k in range(half, views)]
    packed = call(
        functools.partial(pack_kernel, spans, 0, ranks, views),
        [sds((tall[1], width), bf16)] * len(spans),
        [],
        0,
        [slab],
        whole[0][1:],
    )
    moved = {k: swap(packed[k - half], "view", k) for k in farthest_first(views)[:half]}
    whole.append([moved[k] for k in range(half, views)])

    lit, carried, pieces = [], [], []
    for c, count in enumerate(counts):
        outs = [sds((size * count, width), bf16)] * parts + [sds((parts, size * count, width), bf16)]
        if c == 0:
            outs += [sds((ranks, views_all), bf16)]
        waits = [] if c else []
        made = call(
            functools.partial(
                core_kernel, count, 0 if c else head, [0] * half + [tall[0] * c] * half, rows, ranks, views, parts,
                0 if c else groups, len(waits),
            ),
            outs,
            [
                pltpu.VMEM((views, tall[c], width), bf16),
                pltpu.VMEM((width // 128, count * ranks, 128), f32),
            ],
            2 * views_all * count * width * ranks,
            whole[c][::-1] + near[::-1] + carried,
            waits,
        )
        lit += swaps(made[:parts], "light")[::-1]
        pieces.append(made[parts])
        carried = list(made[parts + 1 :])
    back = call(
        functools.partial(back_kernel, 2), [sds((size * lights, width), bf16)] * views, [], 0, pieces, lit[: parts - 1]
    )
    spans = [(k, 0) for k in range(half)] + [(k, c * tall[0]) for c in range(2) for k in range(half, views)]
    wide = -(-max(3 * views_all // 2, lights_all) // 128) * 128
    view_part = call(
        functools.partial(view_kernel, lights, rows, views, spans, view_scale),
        sds((views_all // 2, wide), f32),
        [pltpu.VMEM((views, head + lights * rows, width), bf16)],
        2 * views_all * lights * width * views_all,
        near + whole[0] + whole[1],
    )
    returned = swaps(back, "view")
    sums = call(
        functools.partial(light_kernel, counts, 1, parts, light_scale),
        [sds((lights + views_all // 2, wide), f32)] * parts,
        [pltpu.VMEM((parts, size * count, width), bf16) for count in counts]
        + [pltpu.VMEM((parts, lights, lights_all), f32)],
        2 * lights_all * lights_all * size * width,
        lit + [view_part],
        [returned[1]],
    )
    dealt = call(
        functools.partial(deal_kernel, lights, rows, views),
        [sds((lights + rows, lights_all), f32)] * views,
        [pltpu.VMEM((views, rows, views_all), f32)],
        0,
        swaps(sums, "light")[::-1],
    )
    total = call(sum_kernel, sds((lights + rows, lights_all), f32), [], 0, swaps(dealt, "view")[::-1])
    total = doubled(total, "texel")
    core = call(
        functools.partial(place_kernel, counts),
        sds((ranks // views, lights, columns), bf16),
        [],
        0,
        returned,
    )
    return (total[lights:], core, total[:lights])


def solution(mesh):
    return jax.shard_map(
        body,
        mesh=mesh,
        in_specs=(P("light", "view", "texel"), P("view", None)),
        out_specs=(P("view", None), P("view", "light", "texel"), P("light", None)),
        check_vma=False,
    )
```

```python
import functools

import jax
import jax.numpy as jnp
from jax import lax
from jax.experimental import pallas as pl
from jax.experimental.pallas import tpu as pltpu
from jax.sharding import PartitionSpec as P

VMEM = pl.BlockSpec(memory_space=pltpu.VMEM)
ANY = pl.BlockSpec(memory_space=pl.ANY)
sds = jax.ShapeDtypeStruct
bf16, f32 = jnp.bfloat16, jnp.float32


def swap(value, axis, step):
    return lax.ppermute(value, axis, [(i, i ^ step) for i in range(lax.axis_size(axis))])


def farthest_first(n):
    return list(range(n - 1, -1, -1))


def swaps(values, axis):
    moved = {k: swap(values[k], axis, k) for k in farthest_first(len(values))[:-1]}
    return [values[0]] + [moved[k] for k in range(1, len(values))]


def summed(values):
    total = values[-1]
    for value in values[-2::-1]:
        total = total + value
    return total


def doubled(value, axis):
    step = 1
    while step < lax.axis_size(axis):
        value = value + swap(value, axis, step)
        step *= 2
    return value


def call(kernel, out_shape, scratch, flops, args, unused=()):
    moved = sum(a.size * a.dtype.itemsize for a in list(args) + jax.tree.leaves(out_shape))
    return pl.pallas_call(
        kernel,
        out_shape=out_shape,
        in_specs=[VMEM] * len(args) + [ANY] * len(unused),
        out_specs=jax.tree.map(lambda _: VMEM, out_shape),
        scratch_shapes=scratch,
        compiler_params=pltpu.CompilerParams(vmem_limit_bytes=32 * 1024 * 1024),
        cost_estimate=pl.CostEstimate(flops=flops, bytes_accessed=moved, transcendentals=0),
    )(*args, *unused)


def nt(a, b):
    return lax.dot_general(a, b, (((1,), (1,)), ((), ())), preferred_element_type=f32)


def cut(refs, *counts):
    out, at = [], 0
    for count in counts:
        out.append(refs[at : at + count])
        at += count
    return out + [refs[at:]]


def blank_kernel(out_ref):
    out_ref[...] = jnp.zeros_like(out_ref)


def pack_kernel(spans, groups, ranks, views, slab_ref, *refs):
    me = lax.axis_index("view")
    outs = refs[-len(spans) :]
    rows, columns = slab_ref.shape[1:]
    width = columns // views
    head = []
    if groups:
        deep = rows // groups
        wide = refs[0][...].astype(f32)
        wide = jnp.concatenate([wide[g * deep : (g + 1) * deep] for g in range(groups)], axis=1)
        head = [jnp.pad(wide, ((0, -deep % 8), (0, width - groups * ranks))).astype(bf16)]
    for (k, begin, count), out in zip(spans, outs):
        at = pl.ds(pl.multiple_of((me ^ k) * width, width), width)
        out[...] = jnp.concatenate(head + [slab_ref[l, :, at] for l in range(begin, begin + count)], axis=0)


def core_kernel(lights, head, starts, rows, ranks, views, parts, groups, spare, *refs):
    first = groups > 0
    ins, old, _, light_outs, (pieces, *outs) = cut(refs[:-2], views, 0 if first else 1, spare, parts)
    whole, turned = refs[-2:]
    v, z = lax.axis_index("view"), lax.axis_index("light")
    width = whole.shape[2]
    for i, k in enumerate(farthest_first(views)):
        whole[v ^ k] = ins[i][starts[i] : starts[i] + whole.shape[1], :]
    if first:
        deep = rows // groups
        wide = [whole[k, :head, :].astype(f32)[:deep] for k in range(views)]
        basis = jnp.concatenate([w[:, g * ranks : (g + 1) * ranks] for w in wide for g in range(groups)], axis=0)
        basis = jnp.pad(basis, ((0, 0), (0, 128 - ranks))).T[:ranks].astype(bf16)
    else:
        basis = old[0][...]
    for l in range(lights):
        at = head + l * rows
        page = jnp.concatenate([whole[k, at : at + rows, :] for k in range(views)], axis=0)
        product = jnp.dot(basis, page, preferred_element_type=f32)
        for h in range(width // 128):
            turned[h, l * ranks : (l + 1) * ranks, :] = product[:, h * 128 : (h + 1) * 128]
    size = ranks // parts
    for j in range(parts):
        for h in range(width // 128):
            picked = [turned[h, pl.ds(j * size + r, lights, stride=ranks), :] for r in range(size)]
            pieces[j, :, h * 128 : (h + 1) * 128] = jnp.concatenate(picked, axis=0).astype(bf16)
    for k in range(parts):
        light_outs[k][...] = pieces[z ^ k]
    if first:
        outs[0][...] = basis


def back_kernel(chunks, *refs):
    v, outs = lax.axis_index("view"), refs[-refs[0].shape[0] :]
    for k, out in enumerate(outs):
        out[...] = jnp.concatenate([ref[v ^ k] for ref in refs[:chunks]], axis=0)


def view_kernel(lights, rows, views, spans, scale, *refs):
    ins, (out, whole) = cut(refs, len(spans))
    v = lax.axis_index("view")
    for (k, begin), ref in zip(spans, ins):
        whole[v ^ k, begin : begin + ref.shape[0], :] = ref[...]
    head = whole.shape[1] - lights * rows
    gram = jnp.zeros((views * rows, views * rows), f32)
    for l in range(lights):
        at = head + l * rows
        page = jnp.concatenate([whole[k, at : at + rows, :] for k in range(views)], axis=0)
        gram += nt(page, page)
    gram *= scale
    half = views * rows // 2
    quarters = jnp.concatenate([gram[:half], gram[half:, half:]], axis=1)
    out[...] = jnp.pad(quarters, ((0, 0), (0, out.shape[1] - 3 * half)))


def deal_kernel(lights, rows, views, *refs):
    ins, outs, (blocks,) = cut(refs, len(refs) - views - 1, views)
    v = lax.axis_index("view")
    total = summed([ref[...] for ref in ins])
    light, quarters = total[:lights, : outs[0].shape[1]], total[lights:]
    half = views * rows // 2
    cross = quarters[:, half : 2 * half]
    lower = jnp.concatenate([cross.T, quarters[:, 2 * half : 3 * half]], axis=1)
    gram = jnp.concatenate([quarters[:, : 2 * half], lower], axis=0)
    for k in range(views):
        blocks[k] = gram[k * rows : (k + 1) * rows]
    for k in range(views):
        outs[k][...] = jnp.concatenate([light, blocks[v ^ k]], axis=0)


def sum_kernel(*refs):
    refs[-1][...] = summed([ref[...] for ref in refs[:-1]])


def light_kernel(counts, spare, parts, scale, *refs):
    ins, (view,), _, outs, wholes, (blocks,) = cut(refs, parts * len(counts), 1, spare, parts, len(counts))
    z, lights = lax.axis_index("light"), sum(counts)
    for c, whole in enumerate(wholes):
        for i, k in enumerate(farthest_first(parts)):
            whole[z ^ k] = ins[c * parts + i][...]
    gram = jnp.zeros((parts * lights, parts * lights), f32)
    for r in range(wholes[0].shape[1] // counts[0]):
        page = [wholes[c][k, r * n : (r + 1) * n, :] for k in range(parts) for c, n in enumerate(counts)]
        page = jnp.concatenate(page, axis=0)
        gram += nt(page, page)
    gram *= scale
    for k in range(parts):
        blocks[k] = gram[k * lights : (k + 1) * lights]
    for k in range(parts):
        block = jnp.pad(blocks[z ^ k], ((0, 0), (0, view.shape[1] - parts * lights)))
        outs[k][...] = jnp.concatenate([block, view[...]], axis=0)


def place_kernel(counts, *refs):
    ins, core_ref = refs[:-1], refs[-1]
    v = lax.axis_index("view")
    ranks, width = core_ref.shape[0], ins[0].shape[1]
    for k in range(len(ins)):
        at = pl.ds(pl.multiple_of((v ^ k) * width, width), width)
        for r in range(ranks):
            begin, page = 0, []
            for n in counts:
                page.append(ins[k][begin + r * n : begin + (r + 1) * n, :])
                begin += ranks * n
            core_ref[r, :, at] = jnp.concatenate(page, axis=0)


def body(slab, basis):
    views, parts = lax.axis_size("view"), lax.axis_size("light")
    lights, rows, columns = slab.shape
    ranks = basis.shape[1]
    columns_all = columns * lax.axis_size("texel")
    view_scale = 1.0 / (lights * parts * columns_all)
    light_scale = 1.0 / (ranks * columns_all)
    width = columns // views
    views_all, lights_all = views * rows, parts * lights
    size = ranks // parts
    groups = max(g for g in range(1, width // ranks + 1) if rows % g == 0)
    head = -(-(rows // groups) // 8) * 8

    one = lights * 2 // 5 // 4 * 4
    counts, half = [one, lights - one], views // 2
    tall = [head + one * rows, (lights - one) * rows]

    blank = call(blank_kernel, sds((8, 128), f32), [], 10**9, [])

    spans = [(k, 0, lights if k < half else one) for k in range(views)]
    packed = call(
        functools.partial(pack_kernel, spans, groups, ranks, views),
        [sds((head + count * rows, width), bf16) for _, _, count in spans],
        [],
        0,
        [slab, basis],
        [blank],
    )
    came = swaps(packed, "view")
    near, whole = came[:half], [came[half:]]
    spans = [(k, one, lights - one) for k in range(half, views)]
    packed = call(
        functools.partial(pack_kernel, spans, 0, ranks, views),
        [sds((tall[1], width), bf16)] * len(spans),
        [],
        0,
        [slab],
        whole[0][1:],
    )
    moved = {k: swap(packed[k - half], "view", k) for k in farthest_first(views)[:half]}
    whole.append([moved[k] for k in range(half, views)])

    lit, carried, pieces = [], [], []
    for c, count in enumerate(counts):
        outs = [sds((size * count, width), bf16)] * parts + [sds((parts, size * count, width), bf16)]
        if c == 0:
            outs += [sds((ranks, views_all), bf16)]
        waits = lit[:1] if c else []
        made = call(
            functools.partial(
                core_kernel, count, 0 if c else head, [0] * half + [tall[0] * c] * half, rows, ranks, views, parts,
                0 if c else groups, len(waits),
            ),
            outs,
            [
                pltpu.VMEM((views, tall[c], width), bf16),
                pltpu.VMEM((width // 128, count * ranks, 128), f32),
            ],
            2 * views_all * count * width * ranks,
            whole[c][::-1] + near[::-1] + carried,
            waits,
        )
        lit += swaps(made[:parts], "light")[::-1]
        pieces.append(made[parts])
        carried = list(made[parts + 1 :])
    back = call(
        functools.partial(back_kernel, 2), [sds((size * lights, width), bf16)] * views, [], 0, pieces, lit[: parts - 1]
    )
    spans = [(k, 0) for k in range(half)] + [(k, c * tall[0]) for c in range(2) for k in range(half, views)]
    wide = -(-max(3 * views_all // 2, lights_all) // 128) * 128
    view_part = call(
        functools.partial(view_kernel, lights, rows, views, spans, view_scale),
        sds((views_all // 2, wide), f32),
        [pltpu.VMEM((views, head + lights * rows, width), bf16)],
        2 * views_all * lights * width * views_all,
        near + whole[0] + whole[1],
    )
    returned = swaps(back, "view")
    sums = call(
        functools.partial(light_kernel, counts, 1, parts, light_scale),
        [sds((lights + views_all // 2, wide), f32)] * parts,
        [pltpu.VMEM((parts, size * count, width), bf16) for count in counts]
        + [pltpu.VMEM((parts, lights, lights_all), f32)],
        2 * lights_all * lights_all * size * width,
        lit + [view_part],
        [returned[1]],
    )
    dealt = call(
        functools.partial(deal_kernel, lights, rows, views),
        [sds((lights + rows, lights_all), f32)] * views,
        [pltpu.VMEM((views, rows, views_all), f32)],
        0,
        swaps(sums, "light")[::-1],
    )
    total = call(sum_kernel, sds((lights + rows, lights_all), f32), [], 0, swaps(dealt, "view")[::-1])
    total = doubled(total, "texel")
    core = call(
        functools.partial(place_kernel, counts),
        sds((ranks // views, lights, columns), bf16),
        [],
        0,
        returned,
    )
    return (total[lights:], core, total[:lights])


def solution(mesh):
    return jax.shard_map(
        body,
        mesh=mesh,
        in_specs=(P("light", "view", "texel"), P("view", None)),
        out_specs=(P("view", None), P("view", "light", "texel"), P("light", None)),
        check_vma=False,
    )
```

```python
import functools

import jax
import jax.numpy as jnp
from jax import lax
from jax.experimental import pallas as pl
from jax.experimental.pallas import tpu as pltpu
from jax.sharding import PartitionSpec as P

VMEM = pl.BlockSpec(memory_space=pltpu.VMEM)
ANY = pl.BlockSpec(memory_space=pl.ANY)
sds = jax.ShapeDtypeStruct
bf16, f32 = jnp.bfloat16, jnp.float32


def swap(value, axis, step):
    return lax.ppermute(value, axis, [(i, i ^ step) for i in range(lax.axis_size(axis))])


def farthest_first(n):
    return list(range(n - 1, -1, -1))


def swaps(values, axis):
    moved = {k: swap(values[k], axis, k) for k in farthest_first(len(values))[:-1]}
    return [values[0]] + [moved[k] for k in range(1, len(values))]


def summed(values):
    total = values[-1]
    for value in values[-2::-1]:
        total = total + value
    return total


def call(kernel, out_shape, scratch, flops, args, unused=()):
    moved = sum(a.size * a.dtype.itemsize for a in list(args) + jax.tree.leaves(out_shape))
    return pl.pallas_call(
        kernel,
        out_shape=out_shape,
        in_specs=[VMEM] * len(args) + [ANY] * len(unused),
        out_specs=jax.tree.map(lambda _: VMEM, out_shape),
        scratch_shapes=scratch,
        compiler_params=pltpu.CompilerParams(vmem_limit_bytes=32 * 1024 * 1024),
        cost_estimate=pl.CostEstimate(flops=flops, bytes_accessed=moved, transcendentals=0),
    )(*args, *unused)


def nt(a, b):
    return lax.dot_general(a, b, (((1,), (1,)), ((), ())), preferred_element_type=f32)


def cut(refs, *counts):
    out, at = [], 0
    for count in counts:
        out.append(refs[at : at + count])
        at += count
    return out + [refs[at:]]


def blank_kernel(out_ref):
    out_ref[...] = jnp.zeros_like(out_ref)


def pack_kernel(spans, groups, ranks, views, slab_ref, *refs):
    me = lax.axis_index("view")
    outs = refs[-len(spans) :]
    rows, columns = slab_ref.shape[1:]
    width = columns // views
    head = []
    if groups:
        deep = rows // groups
        wide = refs[0][...].astype(f32)
        wide = jnp.concatenate([wide[g * deep : (g + 1) * deep] for g in range(groups)], axis=1)
        head = [jnp.pad(wide, ((0, -deep % 8), (0, width - groups * ranks))).astype(bf16)]
    for (k, begin, count), out in zip(spans, outs):
        at = pl.ds(pl.multiple_of((me ^ k) * width, width), width)
        out[...] = jnp.concatenate(head + [slab_ref[l, :, at] for l in range(begin, begin + count)], axis=0)


def core_kernel(lights, head, starts, rows, ranks, views, parts, groups, spare, *refs):
    first = groups > 0
    ins, old, _, light_outs, (pieces, *outs) = cut(refs[:-2], views, 0 if first else 1, spare, parts)
    whole, turned = refs[-2:]
    v, z = lax.axis_index("view"), lax.axis_index("light")
    width = whole.shape[2]
    for i, k in enumerate(farthest_first(views)):
        whole[v ^ k] = ins[i][starts[i] : starts[i] + whole.shape[1], :]
    if first:
        deep = rows // groups
        wide = [whole[k, :head, :].astype(f32)[:deep] for k in range(views)]
        basis = jnp.concatenate([w[:, g * ranks : (g + 1) * ranks] for w in wide for g in range(groups)], axis=0)
        basis = jnp.pad(basis, ((0, 0), (0, 128 - ranks))).T[:ranks].astype(bf16)
    else:
        basis = old[0][...]
    for l in range(lights):
        at = head + l * rows
        page = jnp.concatenate([whole[k, at : at + rows, :] for k in range(views)], axis=0)
        product = jnp.dot(basis, page, preferred_element_type=f32)
        for h in range(width // 128):
            turned[h, l * ranks : (l + 1) * ranks, :] = product[:, h * 128 : (h + 1) * 128]
    size = ranks // parts
    for j in range(parts):
        for h in range(width // 128):
            picked = [turned[h, pl.ds(j * size + r, lights, stride=ranks), :] for r in range(size)]
            pieces[j, :, h * 128 : (h + 1) * 128] = jnp.concatenate(picked, axis=0).astype(bf16)
    for k in range(parts):
        light_outs[k][...] = pieces[z ^ k]
    if first:
        outs[0][...] = basis


def back_kernel(chunks, *refs):
    v, outs = lax.axis_index("view"), refs[-refs[0].shape[0] :]
    for k, out in enumerate(outs):
        out[...] = jnp.concatenate([ref[v ^ k] for ref in refs[:chunks]], axis=0)


def view_kernel(lights, rows, views, spans, scale, *refs):
    ins, (out, whole) = cut(refs, len(spans))
    v = lax.axis_index("view")
    for (k, begin), ref in zip(spans, ins):
        whole[v ^ k, begin : begin + ref.shape[0], :] = ref[...]
    head = whole.shape[1] - lights * rows
    gram = jnp.zeros((views * rows, views * rows), f32)
    for l in range(lights):
        at = head + l * rows
        page = jnp.concatenate([whole[k, at : at + rows, :] for k in range(views)], axis=0)
        gram += nt(page, page)
    gram *= scale
    half = views * rows // 2
    left = jnp.zeros((out.shape[1], out.shape[2] - half), f32)
    for p in range(2):
        mine = jnp.concatenate([gram[k * rows : (k + 1) * rows] for k in range(p, views, 2)], axis=0)
        mine = jnp.concatenate([mine[:, :half], mine[:, half:]], axis=0)
        out[p] = jnp.concatenate([left, mine], axis=1)


def deal_light_kernel(lights, parts, keep_ref, came_ref, *refs):
    outs, blocks = refs[:-1], refs[-1]
    z = lax.axis_index("light")
    total = keep_ref[...] + came_ref[...]
    wide = lights * parts
    tall = total.shape[0] // 2
    view = total[:, total.shape[1] - tall :]
    view = jnp.concatenate([view[:tall], view[tall:]], axis=1)
    for k in range(parts):
        light = total[k * lights : (k + 1) * lights, :wide]
        light = jnp.concatenate([light[:, : wide // 2], light[:, wide // 2 :]], axis=0)
        blocks[k] = jnp.concatenate([view, light], axis=1)
    for k in range(parts):
        outs[k][...] = blocks[z ^ k]


def deal_view_kernel(lights, rows, *refs):
    total_ref, outs, blocks = refs[0], refs[1:-1], refs[-1]
    u = lax.axis_index("view") // 2
    total = total_ref[...]
    wide = 2 * rows * len(outs)
    light = total[:, wide:]
    light = jnp.concatenate([light[:lights], light[lights:]], axis=1)
    for m in range(len(outs)):
        blocks[m] = jnp.concatenate([light, total[m * rows : (m + 1) * rows, :wide]], axis=0)
    for m in range(len(outs)):
        outs[m][...] = blocks[u ^ m]


def sum_kernel(*refs):
    refs[-1][...] = summed([ref[...] for ref in refs[:-1]])


def light_kernel(counts, spare, parts, scale, *refs):
    ins, (view,), _, (keep_out, send_out), wholes = cut(refs, parts * len(counts), 1, spare, 2)
    z, lights = lax.axis_index("light"), sum(counts)
    for c, whole in enumerate(wholes):
        for i, k in enumerate(farthest_first(parts)):
            whole[z ^ k] = ins[c * parts + i][...]
    gram = jnp.zeros((parts * lights, parts * lights), f32)
    for r in range(wholes[0].shape[1] // counts[0]):
        page = [wholes[c][k, r * n : (r + 1) * n, :] for k in range(parts) for c, n in enumerate(counts)]
        page = jnp.concatenate(page, axis=0)
        gram += nt(page, page)
    gram *= scale
    gram = jnp.pad(gram, ((0, keep_out.shape[0] - gram.shape[0]), (0, keep_out.shape[1] - gram.shape[1])))
    parity = lax.axis_index("view") % 2
    keep_out[...] = gram + view[parity]
    send_out[...] = gram + view[1 - parity]


def place_kernel(counts, *refs):
    ins, core_ref = refs[:-1], refs[-1]
    v = lax.axis_index("view")
    ranks, width = core_ref.shape[0], ins[0].shape[1]
    for k in range(len(ins)):
        at = pl.ds(pl.multiple_of((v ^ k) * width, width), width)
        for r in range(ranks):
            begin, page = 0, []
            for n in counts:
                page.append(ins[k][begin + r * n : begin + (r + 1) * n, :])
                begin += ranks * n
            core_ref[r, :, at] = jnp.concatenate(page, axis=0)


def body(slab, basis):
    views, parts = lax.axis_size("view"), lax.axis_size("light")
    lights, rows, columns = slab.shape
    ranks = basis.shape[1]
    columns_all = columns * lax.axis_size("texel")
    view_scale = 1.0 / (lights * parts * columns_all)
    light_scale = 1.0 / (ranks * columns_all)
    width = columns // views
    views_all, lights_all = views * rows, parts * lights
    size = ranks // parts
    groups = max(g for g in range(1, width // ranks + 1) if rows % g == 0)
    head = -(-(rows // groups) // 8) * 8

    one = lights * 2 // 5 // 4 * 4
    counts, half = [one, lights - one], views // 2
    tall = [head + one * rows, (lights - one) * rows]

    blank = call(blank_kernel, sds((8, 128), f32), [], 10**9, [])

    spans = [(k, 0, lights if k < half else one) for k in range(views)]
    packed = call(
        functools.partial(pack_kernel, spans, groups, ranks, views),
        [sds((head + count * rows, width), bf16) for _, _, count in spans],
        [],
        0,
        [slab, basis],
        [blank],
    )
    came = swaps(packed, "view")
    near, whole = came[:half], [came[half:]]
    spans = [(k, one, lights - one) for k in range(half, views)]
    packed = call(
        functools.partial(pack_kernel, spans, 0, ranks, views),
        [sds((tall[1], width), bf16)] * len(spans),
        [],
        0,
        [slab],
        whole[0][1:],
    )
    moved = {k: swap(packed[k - half], "view", k) for k in farthest_first(views)[:half]}
    whole.append([moved[k] for k in range(half, views)])

    lit, carried, pieces = [], [], []
    for c, count in enumerate(counts):
        outs = [sds((size * count, width), bf16)] * parts + [sds((parts, size * count, width), bf16)]
        if c == 0:
            outs += [sds((ranks, views_all), bf16)]
        waits = lit[:1] if c else []
        made = call(
            functools.partial(
                core_kernel, count, 0 if c else head, [0] * half + [tall[0] * c] * half, rows, ranks, views, parts,
                0 if c else groups, len(waits),
            ),
            outs,
            [
                pltpu.VMEM((views, tall[c], width), bf16),
                pltpu.VMEM((width // 128, count * ranks, 128), f32),
            ],
            2 * views_all * count * width * ranks,
            whole[c][::-1] + near[::-1] + carried,
            waits,
        )
        lit += swaps(made[:parts], "light")[::-1]
        pieces.append(made[parts])
        carried = list(made[parts + 1 :])
    back = call(
        functools.partial(back_kernel, 2), [sds((size * lights, width), bf16)] * views, [], 0, pieces, lit[: parts - 1]
    )
    spans = [(k, 0) for k in range(half)] + [(k, c * tall[0]) for c in range(2) for k in range(half, views)]
    wide = lights_all + views_all // 2
    both = max(lights_all, views_all)
    view_part = call(
        functools.partial(view_kernel, lights, rows, views, spans, view_scale),
        sds((2, both, wide), f32),
        [pltpu.VMEM((views, head + lights * rows, width), bf16)],
        2 * views_all * lights * width * views_all,
        near + whole[0] + whole[1],
    )
    returned = swaps(back, "view")
    keep, send = call(
        functools.partial(light_kernel, counts, 1, parts, light_scale),
        [sds((both, wide), f32)] * 2,
        [pltpu.VMEM((parts, size * count, width), bf16) for count in counts],
        2 * lights_all * lights_all * size * width,
        lit + [view_part],
        [returned[1]],
    )
    dealt = call(
        functools.partial(deal_light_kernel, lights, parts),
        [sds((views_all // 2, views_all + lights_all // 2), f32)] * parts,
        [pltpu.VMEM((parts, views_all // 2, views_all + lights_all // 2), f32)],
        0,
        [keep, swap(send, "view", 1)],
    )
    total = call(sum_kernel, sds(dealt[0].shape, f32), [], 0, swaps(dealt, "light")[::-1])
    texels, step = lax.axis_size("texel"), 2
    while step < texels:
        total = total + swap(total, "texel", step)
        step *= 2
    dealt = call(
        functools.partial(deal_view_kernel, lights, rows),
        [sds((lights + rows, views_all), f32)] * half,
        [pltpu.VMEM((half, lights + rows, views_all), f32)],
        0,
        [total],
    )
    steps = [(t, m) for t in range(min(2, texels) - 1, -1, -1) for m in range(half - 1, -1, -1)]
    total = summed([dealt[0]] + [swap(dealt[m], ("texel", "view"), t * views + 2 * m) for t, m in steps[:-1]])
    core = call(
        functools.partial(place_kernel, counts),
        sds((ranks // views, lights, columns), bf16),
        [],
        0,
        returned,
    )
    return (total[lights:], core, total[:lights])


def solution(mesh):
    return jax.shard_map(
        body,
        mesh=mesh,
        in_specs=(P("light", "view", "texel"), P("view", None)),
        out_specs=(P("view", None), P("view", "light", "texel"), P("light", None)),
        check_vma=False,
    )
```

```python
import functools

import jax
import jax.numpy as jnp
from jax import lax
from jax.experimental import pallas as pl
from jax.experimental.pallas import tpu as pltpu
from jax.sharding import PartitionSpec as P

VMEM = pl.BlockSpec(memory_space=pltpu.VMEM)
ANY = pl.BlockSpec(memory_space=pl.ANY)
sds = jax.ShapeDtypeStruct
bf16, f32 = jnp.bfloat16, jnp.float32


def swap(value, axis, step):
    return lax.ppermute(value, axis, [(i, i ^ step) for i in range(lax.axis_size(axis))])


def farthest_first(n):
    return list(range(n - 1, -1, -1))


def swaps(values, axis):
    moved = {k: swap(values[k], axis, k) for k in farthest_first(len(values))[:-1]}
    return [values[0]] + [moved[k] for k in range(1, len(values))]


def summed(values):
    total = values[-1]
    for value in values[-2::-1]:
        total = total + value
    return total


def call(kernel, out_shape, scratch, flops, args, unused=()):
    moved = sum(a.size * a.dtype.itemsize for a in list(args) + jax.tree.leaves(out_shape))
    return pl.pallas_call(
        kernel,
        out_shape=out_shape,
        in_specs=[VMEM] * len(args) + [ANY] * len(unused),
        out_specs=jax.tree.map(lambda _: VMEM, out_shape),
        scratch_shapes=scratch,
        compiler_params=pltpu.CompilerParams(vmem_limit_bytes=32 * 1024 * 1024),
        cost_estimate=pl.CostEstimate(flops=flops, bytes_accessed=moved, transcendentals=0),
    )(*args, *unused)


def nt(a, b):
    return lax.dot_general(a, b, (((1,), (1,)), ((), ())), preferred_element_type=f32)


def cut(refs, *counts):
    out, at = [], 0
    for count in counts:
        out.append(refs[at : at + count])
        at += count
    return out + [refs[at:]]


def blank_kernel(out_ref):
    out_ref[...] = jnp.zeros_like(out_ref)


def pack_kernel(spans, groups, ranks, views, slab_ref, *refs):
    me = lax.axis_index("view")
    outs = refs[-len(spans) :]
    rows, columns = slab_ref.shape[1:]
    width = columns // views
    head = []
    if groups:
        deep = rows // groups
        wide = refs[0][...].astype(f32)
        wide = jnp.concatenate([wide[g * deep : (g + 1) * deep] for g in range(groups)], axis=1)
        head = [jnp.pad(wide, ((0, -deep % 8), (0, width - groups * ranks))).astype(bf16)]
    for (k, begin, count), out in zip(spans, outs):
        at = pl.ds(pl.multiple_of((me ^ k) * width, width), width)
        out[...] = jnp.concatenate(head + [slab_ref[l, :, at] for l in range(begin, begin + count)], axis=0)


def core_kernel(lights, head, starts, rows, ranks, views, parts, groups, spare, *refs):
    first = groups > 0
    ins, old, _, light_outs, (pieces, *outs) = cut(refs[:-2], views, 0 if first else 1, spare, parts)
    whole, turned = refs[-2:]
    v, z = lax.axis_index("view"), lax.axis_index("light")
    width = whole.shape[2]
    for i, k in enumerate(farthest_first(views)):
        whole[v ^ k] = ins[i][starts[i] : starts[i] + whole.shape[1], :]
    if first:
        deep = rows // groups
        wide = [whole[k, :head, :].astype(f32)[:deep] for k in range(views)]
        basis = jnp.concatenate([w[:, g * ranks : (g + 1) * ranks] for w in wide for g in range(groups)], axis=0)
        basis = jnp.pad(basis, ((0, 0), (0, 128 - ranks))).T[:ranks].astype(bf16)
    else:
        basis = old[0][...]
    for l in range(lights):
        at = head + l * rows
        page = jnp.concatenate([whole[k, at : at + rows, :] for k in range(views)], axis=0)
        product = jnp.dot(basis, page, preferred_element_type=f32)
        for h in range(width // 128):
            turned[h, l * ranks : (l + 1) * ranks, :] = product[:, h * 128 : (h + 1) * 128]
    size = ranks // parts
    for j in range(parts):
        for h in range(width // 128):
            picked = [turned[h, pl.ds(j * size + r, lights, stride=ranks), :] for r in range(size)]
            pieces[j, :, h * 128 : (h + 1) * 128] = jnp.concatenate(picked, axis=0).astype(bf16)
    for k in range(parts):
        light_outs[k][...] = pieces[z ^ k]
    if first:
        outs[0][...] = basis


def back_kernel(chunks, *refs):
    v, outs = lax.axis_index("view"), refs[-refs[0].shape[0] :]
    for k, out in enumerate(outs):
        out[...] = jnp.concatenate([ref[v ^ k] for ref in refs[:chunks]], axis=0)


def view_kernel(lights, rows, views, spans, scale, *refs):
    ins, (out, whole) = cut(refs, len(spans))
    v = lax.axis_index("view")
    for (k, begin), ref in zip(spans, ins):
        whole[v ^ k, begin : begin + ref.shape[0], :] = ref[...]
    head = whole.shape[1] - lights * rows
    gram = jnp.zeros((views * rows, views * rows), f32)
    for l in range(lights):
        at = head + l * rows
        page = jnp.concatenate([whole[k, at : at + rows, :] for k in range(views)], axis=0)
        gram += nt(page, page)
    gram *= scale
    half = views * rows // 2
    left = jnp.zeros((out.shape[1], out.shape[2] - half), f32)
    for p in range(2):
        mine = jnp.concatenate([gram[k * rows : (k + 1) * rows] for k in range(p, views, 2)], axis=0)
        mine = jnp.concatenate([mine[:, :half], mine[:, half:]], axis=0)
        out[p] = jnp.concatenate([left, mine], axis=1)


def deal_light_kernel(lights, parts, keep_ref, came_ref, *refs):
    outs, blocks = refs[:-1], refs[-1]
    z = lax.axis_index("light")
    total = keep_ref[...] + came_ref[...]
    wide = lights * parts
    tall = total.shape[0] // 2
    view = total[:, total.shape[1] - tall :]
    view = jnp.concatenate([view[:tall], view[tall:]], axis=1)
    for k in range(parts):
        light = total[k * lights : (k + 1) * lights, :wide]
        light = jnp.concatenate([light[:, : wide // 2], light[:, wide // 2 :]], axis=0)
        blocks[k] = jnp.concatenate([view, light], axis=1)
    for k in range(parts):
        outs[k][...] = blocks[z ^ k]


def deal_view_kernel(lights, rows, spare, *refs):
    total_ref, outs, blocks = refs[0], refs[1 + spare : -1], refs[-1]
    u = lax.axis_index("view") // 2
    total = total_ref[...]
    wide = 2 * rows * len(outs)
    light = total[:, wide:]
    light = jnp.concatenate([light[:lights], light[lights:]], axis=1)
    for m in range(len(outs)):
        blocks[m] = jnp.concatenate([light, total[m * rows : (m + 1) * rows, :wide]], axis=0)
    for m in range(len(outs)):
        outs[m][...] = blocks[u ^ m]


def sum_kernel(*refs):
    refs[-1][...] = summed([ref[...] for ref in refs[:-1]])


def light_kernel(counts, spare, parts, scale, *refs):
    ins, (view,), _, (keep_out, send_out), wholes = cut(refs, parts * len(counts), 1, spare, 2)
    z, lights = lax.axis_index("light"), sum(counts)
    for c, whole in enumerate(wholes):
        for i, k in enumerate(farthest_first(parts)):
            whole[z ^ k] = ins[c * parts + i][...]
    gram = jnp.zeros((parts * lights, parts * lights), f32)
    for r in range(wholes[0].shape[1] // counts[0]):
        page = [wholes[c][k, r * n : (r + 1) * n, :] for k in range(parts) for c, n in enumerate(counts)]
        page = jnp.concatenate(page, axis=0)
        gram += nt(page, page)
    gram *= scale
    gram = jnp.pad(gram, ((0, keep_out.shape[0] - gram.shape[0]), (0, keep_out.shape[1] - gram.shape[1])))
    parity = lax.axis_index("view") % 2
    keep_out[...] = gram + view[parity]
    send_out[...] = gram + view[1 - parity]


def place_kernel(counts, *refs):
    ins, core_ref = refs[:-1], refs[-1]
    v = lax.axis_index("view")
    ranks, width = core_ref.shape[0], ins[0].shape[1]
    for k in range(len(ins)):
        at = pl.ds(pl.multiple_of((v ^ k) * width, width), width)
        for r in range(ranks):
            begin, page = 0, []
            for n in counts:
                page.append(ins[k][begin + r * n : begin + (r + 1) * n, :])
                begin += ranks * n
            core_ref[r, :, at] = jnp.concatenate(page, axis=0)


def body(slab, basis):
    views, parts = lax.axis_size("view"), lax.axis_size("light")
    lights, rows, columns = slab.shape
    ranks = basis.shape[1]
    columns_all = columns * lax.axis_size("texel")
    view_scale = 1.0 / (lights * parts * columns_all)
    light_scale = 1.0 / (ranks * columns_all)
    width = columns // views
    views_all, lights_all = views * rows, parts * lights
    size = ranks // parts
    groups = max(g for g in range(1, width // ranks + 1) if rows % g == 0)
    head = -(-(rows // groups) // 8) * 8

    one = lights * 2 // 5 // 4 * 4
    counts, half = [one, lights - one], views // 2
    tall = [head + one * rows, (lights - one) * rows]

    blank = call(blank_kernel, sds((8, 128), f32), [], 10**9, [])

    spans = [(k, 0, lights if k < half else one) for k in range(views)]
    packed = call(
        functools.partial(pack_kernel, spans, groups, ranks, views),
        [sds((head + count * rows, width), bf16) for _, _, count in spans],
        [],
        0,
        [slab, basis],
        [blank],
    )
    came = swaps(packed, "view")
    near, whole = came[:half], [came[half:]]
    spans = [(k, one, lights - one) for k in range(half, views)]
    packed = call(
        functools.partial(pack_kernel, spans, 0, ranks, views),
        [sds((tall[1], width), bf16)] * len(spans),
        [],
        0,
        [slab],
        whole[0][1:],
    )
    moved = {k: swap(packed[k - half], "view", k) for k in farthest_first(views)[:half]}
    whole.append([moved[k] for k in range(half, views)])

    lit, carried, pieces = [], [], []
    for c, count in enumerate(counts):
        outs = [sds((size * count, width), bf16)] * parts + [sds((parts, size * count, width), bf16)]
        if c == 0:
            outs += [sds((ranks, views_all), bf16)]
        waits = lit[:1] if c else []
        made = call(
            functools.partial(
                core_kernel, count, 0 if c else head, [0] * half + [tall[0] * c] * half, rows, ranks, views, parts,
                0 if c else groups, len(waits),
            ),
            outs,
            [
                pltpu.VMEM((views, tall[c], width), bf16),
                pltpu.VMEM((width // 128, count * ranks, 128), f32),
            ],
            2 * views_all * count * width * ranks,
            whole[c][::-1] + near[::-1] + carried,
            waits,
        )
        lit += swaps(made[:parts], "light")[::-1]
        pieces.append(made[parts])
        carried = list(made[parts + 1 :])
    back = call(
        functools.partial(back_kernel, 2), [sds((size * lights, width), bf16)] * views, [], 0, pieces, lit[: parts - 1]
    )
    spans = [(k, 0) for k in range(half)] + [(k, c * tall[0]) for c in range(2) for k in range(half, views)]
    wide = lights_all + views_all // 2
    both = max(lights_all, views_all)
    view_part = call(
        functools.partial(view_kernel, lights, rows, views, spans, view_scale),
        sds((2, both, wide), f32),
        [pltpu.VMEM((views, head + lights * rows, width), bf16)],
        2 * views_all * lights * width * views_all,
        near + whole[0] + whole[1],
    )
    returned = swaps(back, "view")
    keep, send = call(
        functools.partial(light_kernel, counts, 1, parts, light_scale),
        [sds((both, wide), f32)] * 2,
        [pltpu.VMEM((parts, size * count, width), bf16) for count in counts],
        2 * lights_all * lights_all * size * width,
        lit + [view_part],
        [returned[1]],
    )
    dealt = call(
        functools.partial(deal_light_kernel, lights, parts),
        [sds((views_all // 2, views_all + lights_all // 2), f32)] * parts,
        [pltpu.VMEM((parts, views_all // 2, views_all + lights_all // 2), f32)],
        0,
        [keep, swap(send, "view", 1)],
    )
    total = call(sum_kernel, sds(dealt[0].shape, f32), [], 0, swaps(dealt, "light")[::-1])
    texels, step = lax.axis_size("texel"), 2
    while step < texels:
        total = total + swap(total, "texel", step)
        step *= 2
    dealt = call(
        functools.partial(deal_view_kernel, lights, rows, 2),
        [sds((lights + rows, views_all), f32)] * half,
        [pltpu.VMEM((half, lights + rows, views_all), f32)],
        0,
        [total],
        [returned[2], returned[3]],
    )
    steps = [(t, m) for t in range(min(2, texels) - 1, -1, -1) for m in range(half - 1, -1, -1)]
    total = summed([dealt[0]] + [swap(dealt[m], ("texel", "view"), t * views + 2 * m) for t, m in steps[:-1]])
    core = call(
        functools.partial(place_kernel, counts),
        sds((ranks // views, lights, columns), bf16),
        [],
        0,
        returned,
    )
    return (total[lights:], core, total[:lights])


def solution(mesh):
    return jax.shard_map(
        body,
        mesh=mesh,
        in_specs=(P("light", "view", "texel"), P("view", None)),
        out_specs=(P("view", None), P("view", "light", "texel"), P("light", None)),
        check_vma=False,
    )
```

```python
import functools

import jax
import jax.numpy as jnp
from jax import lax
from jax.experimental import pallas as pl
from jax.experimental.pallas import tpu as pltpu
from jax.sharding import PartitionSpec as P

VMEM = pl.BlockSpec(memory_space=pltpu.VMEM)
ANY = pl.BlockSpec(memory_space=pl.ANY)
sds = jax.ShapeDtypeStruct
bf16, f32 = jnp.bfloat16, jnp.float32


def swap(value, axis, step):
    return lax.ppermute(value, axis, [(i, i ^ step) for i in range(lax.axis_size(axis))])


def farthest_first(n):
    return list(range(n - 1, -1, -1))


def middle_first(n):
    return [n // 2] + [k for k in range(n - 1, -1, -1) if k != n // 2]


def swaps(values, axis):
    moved = {k: swap(values[k], axis, k) for k in farthest_first(len(values))[:-1]}
    return [values[0]] + [moved[k] for k in range(1, len(values))]


def summed(values):
    total = values[-1]
    for value in values[-2::-1]:
        total = total + value
    return total


def doubled(value, axis):
    step = 1
    while step < lax.axis_size(axis):
        value = value + swap(value, axis, step)
        step *= 2
    return value


def call(kernel, out_shape, scratch, flops, args, unused=()):
    moved = sum(a.size * a.dtype.itemsize for a in list(args) + jax.tree.leaves(out_shape))
    return pl.pallas_call(
        kernel,
        out_shape=out_shape,
        in_specs=[VMEM] * len(args) + [ANY] * len(unused),
        out_specs=jax.tree.map(lambda _: VMEM, out_shape),
        scratch_shapes=scratch,
        compiler_params=pltpu.CompilerParams(vmem_limit_bytes=32 * 1024 * 1024),
        cost_estimate=pl.CostEstimate(flops=flops, bytes_accessed=moved, transcendentals=0),
    )(*args, *unused)


def nt(a, b):
    return lax.dot_general(a, b, (((1,), (1,)), ((), ())), preferred_element_type=f32)


def cut(refs, *counts):
    out, at = [], 0
    for count in counts:
        out.append(refs[at : at + count])
        at += count
    return out + [refs[at:]]


def blank_kernel(out_ref):
    out_ref[...] = jnp.zeros_like(out_ref)


def pack_kernel(spans, groups, ranks, views, slab_ref, *refs):
    me = lax.axis_index("view")
    outs = refs[-len(spans) :]
    rows, columns = slab_ref.shape[1:]
    width = columns // views
    head = []
    if groups:
        deep = rows // groups
        wide = refs[0][...].astype(f32)
        wide = jnp.concatenate([wide[g * deep : (g + 1) * deep] for g in range(groups)], axis=1)
        head = [jnp.pad(wide, ((0, -deep % 8), (0, width - groups * ranks))).astype(bf16)]
    for (k, begin, count), out in zip(spans, outs):
        at = pl.ds(pl.multiple_of((me ^ k) * width, width), width)
        out[...] = jnp.concatenate(head + [slab_ref[l, :, at] for l in range(begin, begin + count)], axis=0)


def core_kernel(lights, head, starts, rows, ranks, views, parts, groups, spare, *refs):
    first = groups > 0
    ins, old, _, light_outs, (pieces, *outs) = cut(refs[:-2], views, 0 if first else 1, spare, parts)
    whole, turned = refs[-2:]
    v, z = lax.axis_index("view"), lax.axis_index("light")
    width = whole.shape[2]
    for i, k in enumerate(farthest_first(views)):
        whole[v ^ k] = ins[i][starts[i] : starts[i] + whole.shape[1], :]
    if first:
        deep = rows // groups
        wide = [whole[k, :head, :].astype(f32)[:deep] for k in range(views)]
        basis = jnp.concatenate([w[:, g * ranks : (g + 1) * ranks] for w in wide for g in range(groups)], axis=0)
        basis = jnp.pad(basis, ((0, 0), (0, 128 - ranks))).T[:ranks].astype(bf16)
    else:
        basis = old[0][...]
    for l in range(lights):
        at = head + l * rows
        page = jnp.concatenate([whole[k, at : at + rows, :] for k in range(views)], axis=0)
        product = jnp.dot(basis, page, preferred_element_type=f32)
        for h in range(width // 128):
            turned[h, l * ranks : (l + 1) * ranks, :] = product[:, h * 128 : (h + 1) * 128]
    size = ranks // parts
    for j in range(parts):
        for h in range(width // 128):
            picked = [turned[h, pl.ds(j * size + r, lights, stride=ranks), :] for r in range(size)]
            pieces[j, :, h * 128 : (h + 1) * 128] = jnp.concatenate(picked, axis=0).astype(bf16)
    for k in range(parts):
        light_outs[k][...] = pieces[z ^ k]
    if first:
        outs[0][...] = basis


def back_kernel(chunks, *refs):
    v, outs = lax.axis_index("view"), refs[-refs[0].shape[0] :]
    for k, out in enumerate(outs):
        out[...] = jnp.concatenate([ref[v ^ k] for ref in refs[:chunks]], axis=0)


def view_kernel(lights, rows, views, spans, scale, *refs):
    ins, (out, whole) = cut(refs, len(spans))
    v = lax.axis_index("view")
    for (k, begin), ref in zip(spans, ins):
        whole[v ^ k, begin : begin + ref.shape[0], :] = ref[...]
    head = whole.shape[1] - lights * rows
    gram = jnp.zeros((views * rows, views * rows), f32)
    for l in range(lights):
        at = head + l * rows
        page = jnp.concatenate([whole[k, at : at + rows, :] for k in range(views)], axis=0)
        gram += nt(page, page)
    gram *= scale
    half = views * rows // 2
    quarters = jnp.concatenate([gram[:half], gram[half:, half:]], axis=1)
    out[...] = jnp.pad(quarters, ((0, 0), (0, out.shape[1] - 3 * half)))


def deal_kernel(lights, rows, views, *refs):
    ins, outs, (blocks,) = cut(refs, len(refs) - views - 1, views)
    v = lax.axis_index("view")
    total = summed([ref[...] for ref in ins])
    light, quarters = total[:lights, : outs[0].shape[1]], total[lights:]
    half = views * rows // 2
    cross = quarters[:, half : 2 * half]
    lower = jnp.concatenate([cross.T, quarters[:, 2 * half : 3 * half]], axis=1)
    gram = jnp.concatenate([quarters[:, : 2 * half], lower], axis=0)
    for k in range(views):
        blocks[k] = gram[k * rows : (k + 1) * rows]
    for k in range(views):
        outs[k][...] = jnp.concatenate([light, blocks[v ^ k]], axis=0)


def sum_kernel(*refs):
    refs[-1][...] = summed([ref[...] for ref in refs[:-1]])


def light_kernel(counts, spare, parts, scale, *refs):
    ins, (view,), _, outs, wholes, (blocks,) = cut(refs, parts * len(counts), 1, spare, parts, len(counts))
    z, lights = lax.axis_index("light"), sum(counts)
    for c, whole in enumerate(wholes):
        for i, k in enumerate(middle_first(parts)):
            whole[z ^ k] = ins[c * parts + i][...]
    gram = jnp.zeros((parts * lights, parts * lights), f32)
    for r in range(wholes[0].shape[1] // counts[0]):
        page = [wholes[c][k, r * n : (r + 1) * n, :] for k in range(parts) for c, n in enumerate(counts)]
        page = jnp.concatenate(page, axis=0)
        gram += nt(page, page)
    gram *= scale
    for k in range(parts):
        blocks[k] = gram[k * lights : (k + 1) * lights]
    for k in range(parts):
        block = jnp.pad(blocks[z ^ k], ((0, 0), (0, view.shape[1] - parts * lights)))
        outs[k][...] = jnp.concatenate([block, view[...]], axis=0)


def place_kernel(counts, *refs):
    ins, core_ref = refs[:-1], refs[-1]
    v = lax.axis_index("view")
    ranks, width = core_ref.shape[0], ins[0].shape[1]
    for k in range(len(ins)):
        at = pl.ds(pl.multiple_of((v ^ k) * width, width), width)
        for r in range(ranks):
            begin, page = 0, []
            for n in counts:
                page.append(ins[k][begin + r * n : begin + (r + 1) * n, :])
                begin += ranks * n
            core_ref[r, :, at] = jnp.concatenate(page, axis=0)


def body(slab, basis):
    views, parts = lax.axis_size("view"), lax.axis_size("light")
    lights, rows, columns = slab.shape
    ranks = basis.shape[1]
    columns_all = columns * lax.axis_size("texel")
    view_scale = 1.0 / (lights * parts * columns_all)
    light_scale = 1.0 / (ranks * columns_all)
    width = columns // views
    views_all, lights_all = views * rows, parts * lights
    size = ranks // parts
    groups = max(g for g in range(1, width // ranks + 1) if rows % g == 0)
    head = -(-(rows // groups) // 8) * 8

    one = lights * 2 // 5 // 4 * 4
    counts, half = [one, lights - one], views // 2
    tall = [head + one * rows, (lights - one) * rows]

    blank = call(blank_kernel, sds((8, 128), f32), [], 10**9, [])

    spans = [(k, 0, lights if k < half else one) for k in range(views)]
    packed = call(
        functools.partial(pack_kernel, spans, groups, ranks, views),
        [sds((head + count * rows, width), bf16) for _, _, count in spans],
        [],
        0,
        [slab, basis],
        [blank],
    )
    came = swaps(packed, "view")
    near, whole = came[:half], [came[half:]]
    spans = [(k, one, lights - one) for k in range(half, views)]
    packed = call(
        functools.partial(pack_kernel, spans, 0, ranks, views),
        [sds((tall[1], width), bf16)] * len(spans),
        [],
        0,
        [slab],
        whole[0][1:],
    )
    moved = {k: swap(packed[k - half], "view", k) for k in farthest_first(views)[:half]}
    whole.append([moved[k] for k in range(half, views)])

    lit, carried, pieces = [], [], []
    for c, count in enumerate(counts):
        outs = [sds((size * count, width), bf16)] * parts + [sds((parts, size * count, width), bf16)]
        if c == 0:
            outs += [sds((ranks, views_all), bf16)]
        waits = lit[:1] if c else []
        made = call(
            functools.partial(
                core_kernel, count, 0 if c else head, [0] * half + [tall[0] * c] * half, rows, ranks, views, parts,
                0 if c else groups, len(waits),
            ),
            outs,
            [
                pltpu.VMEM((views, tall[c], width), bf16),
                pltpu.VMEM((width // 128, count * ranks, 128), f32),
            ],
            2 * views_all * count * width * ranks,
            whole[c][::-1] + near[::-1] + carried,
            waits,
        )
        got = swaps(made[:parts], "light")
        lit += [got[k] for k in middle_first(parts)]
        pieces.append(made[parts])
        carried = list(made[parts + 1 :])
    back = call(
        functools.partial(back_kernel, 2), [sds((size * lights, width), bf16)] * views, [], 0, pieces, lit[: parts - 1]
    )
    spans = [(k, 0) for k in range(half)] + [(k, c * tall[0]) for c in range(2) for k in range(half, views)]
    wide = -(-max(3 * views_all // 2, lights_all) // 128) * 128
    view_part = call(
        functools.partial(view_kernel, lights, rows, views, spans, view_scale),
        sds((views_all // 2, wide), f32),
        [pltpu.VMEM((views, head + lights * rows, width), bf16)],
        2 * views_all * lights * width * views_all,
        near + whole[0] + whole[1],
    )
    returned = swaps(back, "view")
    sums = call(
        functools.partial(light_kernel, counts, 1, parts, light_scale),
        [sds((lights + views_all // 2, wide), f32)] * parts,
        [pltpu.VMEM((parts, size * count, width), bf16) for count in counts]
        + [pltpu.VMEM((parts, lights, lights_all), f32)],
        2 * lights_all * lights_all * size * width,
        lit + [view_part],
        [returned[1]],
    )
    got = swaps(sums, "light")
    dealt = call(
        functools.partial(deal_kernel, lights, rows, views),
        [sds((lights + rows, lights_all), f32)] * views,
        [pltpu.VMEM((views, rows, views_all), f32)],
        0,
        [got[k] for k in middle_first(parts)],
    )
    total = call(sum_kernel, sds((lights + rows, lights_all), f32), [], 0, swaps(dealt, "view")[::-1])
    total = doubled(total, "texel")
    core = call(
        functools.partial(place_kernel, counts),
        sds((ranks // views, lights, columns), bf16),
        [],
        0,
        returned,
    )
    return (total[lights:], core, total[:lights])


def solution(mesh):
    return jax.shard_map(
        body,
        mesh=mesh,
        in_specs=(P("light", "view", "texel"), P("view", None)),
        out_specs=(P("view", None), P("view", "light", "texel"), P("light", None)),
        check_vma=False,
    )
```

```python
import functools

import jax
import jax.numpy as jnp
from jax import lax
from jax.experimental import pallas as pl
from jax.experimental.pallas import tpu as pltpu
from jax.sharding import PartitionSpec as P

VMEM = pl.BlockSpec(memory_space=pltpu.VMEM)
ANY = pl.BlockSpec(memory_space=pl.ANY)
sds = jax.ShapeDtypeStruct
bf16, f32 = jnp.bfloat16, jnp.float32


def swap(value, axis, step):
    return lax.ppermute(value, axis, [(i, i ^ step) for i in range(lax.axis_size(axis))])


def farthest_first(n):
    return list(range(n - 1, -1, -1))


def middle_first(n):
    return [n // 2] + [k for k in range(n - 1, -1, -1) if k != n // 2]


def swaps(values, axis):
    moved = {k: swap(values[k], axis, k) for k in farthest_first(len(values))[:-1]}
    return [values[0]] + [moved[k] for k in range(1, len(values))]


def summed(values):
    total = values[-1]
    for value in values[-2::-1]:
        total = total + value
    return total


def doubled(value, axis):
    step = 1
    while step < lax.axis_size(axis):
        value = value + swap(value, axis, step)
        step *= 2
    return value


def call(kernel, out_shape, scratch, flops, args, unused=()):
    moved = sum(a.size * a.dtype.itemsize for a in list(args) + jax.tree.leaves(out_shape))
    return pl.pallas_call(
        kernel,
        out_shape=out_shape,
        in_specs=[VMEM] * len(args) + [ANY] * len(unused),
        out_specs=jax.tree.map(lambda _: VMEM, out_shape),
        scratch_shapes=scratch,
        compiler_params=pltpu.CompilerParams(vmem_limit_bytes=32 * 1024 * 1024),
        cost_estimate=pl.CostEstimate(flops=flops, bytes_accessed=moved, transcendentals=0),
    )(*args, *unused)


def nt(a, b):
    return lax.dot_general(a, b, (((1,), (1,)), ((), ())), preferred_element_type=f32)


def cut(refs, *counts):
    out, at = [], 0
    for count in counts:
        out.append(refs[at : at + count])
        at += count
    return out + [refs[at:]]


def blank_kernel(out_ref):
    out_ref[...] = jnp.zeros_like(out_ref)


def pack_kernel(spans, groups, ranks, views, slab_ref, *refs):
    me = lax.axis_index("view")
    outs = refs[-len(spans) :]
    rows, columns = slab_ref.shape[1:]
    width = columns // views
    head = []
    if groups:
        deep = rows // groups
        wide = refs[0][...].astype(f32)
        wide = jnp.concatenate([wide[g * deep : (g + 1) * deep] for g in range(groups)], axis=1)
        head = [jnp.pad(wide, ((0, -deep % 8), (0, width - groups * ranks))).astype(bf16)]
    for (k, begin, count), out in zip(spans, outs):
        at = pl.ds(pl.multiple_of((me ^ k) * width, width), width)
        out[...] = jnp.concatenate(head + [slab_ref[l, :, at] for l in range(begin, begin + count)], axis=0)


def core_kernel(lights, head, starts, rows, ranks, views, parts, groups, spare, *refs):
    first = groups > 0
    ins, old, _, light_outs, (pieces, *outs) = cut(refs[:-2], views, 0 if first else 1, spare, parts)
    whole, turned = refs[-2:]
    v, z = lax.axis_index("view"), lax.axis_index("light")
    width = whole.shape[2]
    for i, k in enumerate(middle_first(views)):
        whole[v ^ k] = ins[i][starts[i] : starts[i] + whole.shape[1], :]
    if first:
        deep = rows // groups
        wide = [whole[k, :head, :].astype(f32)[:deep] for k in range(views)]
        basis = jnp.concatenate([w[:, g * ranks : (g + 1) * ranks] for w in wide for g in range(groups)], axis=0)
        basis = jnp.pad(basis, ((0, 0), (0, 128 - ranks))).T[:ranks].astype(bf16)
    else:
        basis = old[0][...]
    for l in range(lights):
        at = head + l * rows
        page = jnp.concatenate([whole[k, at : at + rows, :] for k in range(views)], axis=0)
        product = jnp.dot(basis, page, preferred_element_type=f32)
        for h in range(width // 128):
            turned[h, l * ranks : (l + 1) * ranks, :] = product[:, h * 128 : (h + 1) * 128]
    size = ranks // parts
    for j in range(parts):
        for h in range(width // 128):
            picked = [turned[h, pl.ds(j * size + r, lights, stride=ranks), :] for r in range(size)]
            pieces[j, :, h * 128 : (h + 1) * 128] = jnp.concatenate(picked, axis=0).astype(bf16)
    for k in range(parts):
        light_outs[k][...] = pieces[z ^ k]
    if first:
        outs[0][...] = basis


def back_kernel(chunks, *refs):
    v, outs = lax.axis_index("view"), refs[-refs[0].shape[0] :]
    for k, out in enumerate(outs):
        out[...] = jnp.concatenate([ref[v ^ k] for ref in refs[:chunks]], axis=0)


def view_kernel(lights, rows, views, spans, scale, *refs):
    ins, (out, whole) = cut(refs, len(spans))
    v = lax.axis_index("view")
    for (k, begin), ref in zip(spans, ins):
        whole[v ^ k, begin : begin + ref.shape[0], :] = ref[...]
    head = whole.shape[1] - lights * rows
    gram = jnp.zeros((views * rows, views * rows), f32)
    for l in range(lights):
        at = head + l * rows
        page = jnp.concatenate([whole[k, at : at + rows, :] for k in range(views)], axis=0)
        gram += nt(page, page)
    gram *= scale
    half = views * rows // 2
    quarters = jnp.concatenate([gram[:half], gram[half:, half:]], axis=1)
    out[...] = jnp.pad(quarters, ((0, 0), (0, out.shape[1] - 3 * half)))


def deal_kernel(lights, rows, views, *refs):
    ins, outs, (blocks,) = cut(refs, len(refs) - views - 1, views)
    v = lax.axis_index("view")
    total = summed([ref[...] for ref in ins])
    light, quarters = total[:lights, : outs[0].shape[1]], total[lights:]
    half = views * rows // 2
    cross = quarters[:, half : 2 * half]
    lower = jnp.concatenate([cross.T, quarters[:, 2 * half : 3 * half]], axis=1)
    gram = jnp.concatenate([quarters[:, : 2 * half], lower], axis=0)
    for k in range(views):
        blocks[k] = gram[k * rows : (k + 1) * rows]
    for k in range(views):
        outs[k][...] = jnp.concatenate([light, blocks[v ^ k]], axis=0)


def sum_kernel(*refs):
    refs[-1][...] = summed([ref[...] for ref in refs[:-1]])


def light_kernel(counts, spare, parts, scale, *refs):
    ins, (view,), _, outs, wholes, (blocks,) = cut(refs, parts * len(counts), 1, spare, parts, len(counts))
    z, lights = lax.axis_index("light"), sum(counts)
    for c, whole in enumerate(wholes):
        for i, k in enumerate(farthest_first(parts)):
            whole[z ^ k] = ins[c * parts + i][...]
    gram = jnp.zeros((parts * lights, parts * lights), f32)
    for r in range(wholes[0].shape[1] // counts[0]):
        page = [wholes[c][k, r * n : (r + 1) * n, :] for k in range(parts) for c, n in enumerate(counts)]
        page = jnp.concatenate(page, axis=0)
        gram += nt(page, page)
    gram *= scale
    for k in range(parts):
        blocks[k] = gram[k * lights : (k + 1) * lights]
    for k in range(parts):
        block = jnp.pad(blocks[z ^ k], ((0, 0), (0, view.shape[1] - parts * lights)))
        outs[k][...] = jnp.concatenate([block, view[...]], axis=0)


def place_kernel(counts, *refs):
    ins, core_ref = refs[:-1], refs[-1]
    v = lax.axis_index("view")
    ranks, width = core_ref.shape[0], ins[0].shape[1]
    for k in range(len(ins)):
        at = pl.ds(pl.multiple_of((v ^ k) * width, width), width)
        for r in range(ranks):
            begin, page = 0, []
            for n in counts:
                page.append(ins[k][begin + r * n : begin + (r + 1) * n, :])
                begin += ranks * n
            core_ref[r, :, at] = jnp.concatenate(page, axis=0)


def body(slab, basis):
    views, parts = lax.axis_size("view"), lax.axis_size("light")
    lights, rows, columns = slab.shape
    ranks = basis.shape[1]
    columns_all = columns * lax.axis_size("texel")
    view_scale = 1.0 / (lights * parts * columns_all)
    light_scale = 1.0 / (ranks * columns_all)
    width = columns // views
    views_all, lights_all = views * rows, parts * lights
    size = ranks // parts
    groups = max(g for g in range(1, width // ranks + 1) if rows % g == 0)
    head = -(-(rows // groups) // 8) * 8

    one = lights * 2 // 5 // 4 * 4
    counts, half = [one, lights - one], views // 2
    tall = [head + one * rows, (lights - one) * rows]

    blank = call(blank_kernel, sds((8, 128), f32), [], 10**9, [])

    spans = [(k, 0, lights if k < half else one) for k in range(views)]
    packed = call(
        functools.partial(pack_kernel, spans, groups, ranks, views),
        [sds((head + count * rows, width), bf16) for _, _, count in spans],
        [],
        0,
        [slab, basis],
        [blank],
    )
    came = swaps(packed, "view")
    near, whole = came[:half], [came[half:]]
    spans = [(k, one, lights - one) for k in range(half, views)]
    packed = call(
        functools.partial(pack_kernel, spans, 0, ranks, views),
        [sds((tall[1], width), bf16)] * len(spans),
        [],
        0,
        [slab],
        whole[0][:1],
    )
    moved = {k: swap(packed[k - half], "view", k) for k in farthest_first(views)[:half]}
    whole.append([moved[k] for k in range(half, views)])

    lit, carried, pieces = [], [], []
    for c, count in enumerate(counts):
        outs = [sds((size * count, width), bf16)] * parts + [sds((parts, size * count, width), bf16)]
        if c == 0:
            outs += [sds((ranks, views_all), bf16)]
        waits = lit[:1] if c else []
        made = call(
            functools.partial(
                core_kernel, count, 0 if c else head, [0 if k >= half else tall[0] * c for k in middle_first(views)], rows, ranks, views, parts,
                0 if c else groups, len(waits),
            ),
            outs,
            [
                pltpu.VMEM((views, tall[c], width), bf16),
                pltpu.VMEM((width // 128, count * ranks, 128), f32),
            ],
            2 * views_all * count * width * ranks,
            [(near + whole[c])[k] for k in middle_first(views)] + carried,
            waits,
        )
        lit += swaps(made[:parts], "light")[::-1]
        pieces.append(made[parts])
        carried = list(made[parts + 1 :])
    back = call(
        functools.partial(back_kernel, 2), [sds((size * lights, width), bf16)] * views, [], 0, pieces, lit[: parts - 1]
    )
    spans = [(k, 0) for k in range(half)] + [(k, c * tall[0]) for c in range(2) for k in range(half, views)]
    wide = -(-max(3 * views_all // 2, lights_all) // 128) * 128
    view_part = call(
        functools.partial(view_kernel, lights, rows, views, spans, view_scale),
        sds((views_all // 2, wide), f32),
        [pltpu.VMEM((views, head + lights * rows, width), bf16)],
        2 * views_all * lights * width * views_all,
        near + whole[0] + whole[1],
    )
    returned = swaps(back, "view")
    sums = call(
        functools.partial(light_kernel, counts, 1, parts, light_scale),
        [sds((lights + views_all // 2, wide), f32)] * parts,
        [pltpu.VMEM((parts, size * count, width), bf16) for count in counts]
        + [pltpu.VMEM((parts, lights, lights_all), f32)],
        2 * lights_all * lights_all * size * width,
        lit + [view_part],
        [returned[1]],
    )
    got = swaps(sums, "light")
    dealt = call(
        functools.partial(deal_kernel, lights, rows, views),
        [sds((lights + rows, lights_all), f32)] * views,
        [pltpu.VMEM((views, rows, views_all), f32)],
        0,
        [got[k] for k in middle_first(parts)],
    )
    got = swaps(dealt, "view")
    got = [got[k] for k in middle_first(views)]
    total = call(sum_kernel, sds((lights + rows, lights_all), f32), [], 0, got)
    total = doubled(total, "texel")
    core = call(
        functools.partial(place_kernel, counts),
        sds((ranks // views, lights, columns), bf16),
        [],
        0,
        returned,
    )
    return (total[lights:], core, total[:lights])


def solution(mesh):
    return jax.shard_map(
        body,
        mesh=mesh,
        in_specs=(P("light", "view", "texel"), P("view", None)),
        out_specs=(P("view", None), P("view", "light", "texel"), P("light", None)),
        check_vma=False,
    )
```

```python
import functools

import jax
import jax.numpy as jnp
from jax import lax
from jax.experimental import pallas as pl
from jax.experimental.pallas import tpu as pltpu
from jax.sharding import PartitionSpec as P

VMEM = pl.BlockSpec(memory_space=pltpu.VMEM)
ANY = pl.BlockSpec(memory_space=pl.ANY)
sds = jax.ShapeDtypeStruct
bf16, f32 = jnp.bfloat16, jnp.float32


def swap(value, axis, step):
    return lax.ppermute(value, axis, [(i, i ^ step) for i in range(lax.axis_size(axis))])


def farthest_first(n):
    return list(range(n - 1, -1, -1))


def swaps(values, axis):
    moved = {k: swap(values[k], axis, k) for k in farthest_first(len(values))[:-1]}
    return [values[0]] + [moved[k] for k in range(1, len(values))]


def summed(values):
    total = values[-1]
    for value in values[-2::-1]:
        total = total + value
    return total


def doubled(value, axis):
    step = 1
    while step < lax.axis_size(axis):
        value = value + swap(value, axis, step)
        step *= 2
    return value


def call(kernel, out_shape, scratch, flops, args, unused=()):
    moved = sum(a.size * a.dtype.itemsize for a in list(args) + jax.tree.leaves(out_shape))
    return pl.pallas_call(
        kernel,
        out_shape=out_shape,
        in_specs=[VMEM] * len(args) + [ANY] * len(unused),
        out_specs=jax.tree.map(lambda _: VMEM, out_shape),
        scratch_shapes=scratch,
        compiler_params=pltpu.CompilerParams(vmem_limit_bytes=32 * 1024 * 1024),
        cost_estimate=pl.CostEstimate(flops=flops, bytes_accessed=moved, transcendentals=0),
    )(*args, *unused)


def nt(a, b):
    return lax.dot_general(a, b, (((1,), (1,)), ((), ())), preferred_element_type=f32)


def cut(refs, *counts):
    out, at = [], 0
    for count in counts:
        out.append(refs[at : at + count])
        at += count
    return out + [refs[at:]]


def blank_kernel(out_ref):
    out_ref[...] = jnp.zeros_like(out_ref)


def pack_kernel(spans, groups, ranks, views, slab_ref, *refs):
    me = lax.axis_index("view")
    outs = refs[-len(spans) :]
    rows, columns = slab_ref.shape[1:]
    width = columns // views
    head = []
    if groups:
        deep = rows // groups
        wide = refs[0][...].astype(f32)
        wide = jnp.concatenate([wide[g * deep : (g + 1) * deep] for g in range(groups)], axis=1)
        head = [jnp.pad(wide, ((0, -deep % 16), (0, width - groups * ranks))).astype(bf16)]
    for (k, begin, count), out in zip(spans, outs):
        at = pl.ds(pl.multiple_of((me ^ k) * width, width), width)
        out[...] = jnp.concatenate(head + [slab_ref[l, :, at] for l in range(begin, begin + count)], axis=0)


def core_kernel(lights, head, starts, rows, ranks, views, parts, groups, spare, *refs):
    first = groups > 0
    ins, old, _, light_outs, (pieces, *outs) = cut(refs[:-2], views, 0 if first else 1, spare, parts)
    whole, turned = refs[-2:]
    v, z = lax.axis_index("view"), lax.axis_index("light")
    width = whole.shape[2]
    for i, k in enumerate(farthest_first(views)):
        whole[v ^ k] = ins[i][starts[i] : starts[i] + whole.shape[1], :]
    if first:
        deep = rows // groups
        wide = [whole[k, :head, :].astype(f32)[:deep] for k in range(views)]
        basis = jnp.concatenate([w[:, g * ranks : (g + 1) * ranks] for w in wide for g in range(groups)], axis=0)
        basis = jnp.pad(basis, ((0, 0), (0, 128 - ranks))).T[:ranks].astype(bf16)
    else:
        basis = old[0][...]
    for l in range(lights):
        at = head + l * rows
        page = jnp.concatenate([whole[k, at : at + rows, :] for k in range(views)], axis=0)
        product = jnp.dot(basis, page, preferred_element_type=f32)
        for h in range(width // 128):
            turned[h, l * ranks : (l + 1) * ranks, :] = product[:, h * 128 : (h + 1) * 128]
    size = ranks // parts
    for j in range(parts):
        for h in range(width // 128):
            picked = [turned[h, pl.ds(j * size + r, lights, stride=ranks), :] for r in range(size)]
            pieces[j, :, h * 128 : (h + 1) * 128] = jnp.concatenate(picked, axis=0).astype(bf16)
    for k in range(parts):
        light_outs[k][...] = pieces[z ^ k]
    if first:
        outs[0][...] = basis


def back_kernel(chunks, *refs):
    v, outs = lax.axis_index("view"), refs[-refs[0].shape[0] :]
    for k, out in enumerate(outs):
        out[...] = jnp.concatenate([ref[v ^ k] for ref in refs[:chunks]], axis=0)


def view_kernel(lights, rows, views, spans, scale, *refs):
    ins, (out, whole) = cut(refs, len(spans))
    v = lax.axis_index("view")
    for (k, begin), ref in zip(spans, ins):
        whole[v ^ k, begin : begin + ref.shape[0], :] = ref[...]
    head = whole.shape[1] - lights * rows
    gram = jnp.zeros((views * rows, views * rows), f32)
    for l in range(lights):
        at = head + l * rows
        page = jnp.concatenate([whole[k, at : at + rows, :] for k in range(views)], axis=0)
        gram += nt(page, page)
    gram *= scale
    half = views * rows // 2
    quarters = jnp.concatenate([gram[:half], gram[half:, half:]], axis=1)
    out[...] = jnp.pad(quarters, ((0, 0), (0, out.shape[1] - 3 * half)))


def deal_kernel(lights, rows, views, *refs):
    ins, outs, (blocks,) = cut(refs, len(refs) - views - 1, views)
    v = lax.axis_index("view")
    total = summed([ref[...] for ref in ins])
    light, quarters = total[:lights, : outs[0].shape[1]], total[lights:]
    half = views * rows // 2
    cross = quarters[:, half : 2 * half]
    lower = jnp.concatenate([cross.T, quarters[:, 2 * half : 3 * half]], axis=1)
    gram = jnp.concatenate([quarters[:, : 2 * half], lower], axis=0)
    for k in range(views):
        blocks[k] = gram[k * rows : (k + 1) * rows]
    for k in range(views):
        outs[k][...] = jnp.concatenate([light, blocks[v ^ k]], axis=0)


def sum_kernel(*refs):
    refs[-1][...] = summed([ref[...] for ref in refs[:-1]])


def light_kernel(counts, spare, parts, scale, *refs):
    ins, (view,), _, outs, wholes, (blocks,) = cut(refs, parts * len(counts), 1, spare, parts, len(counts))
    z, lights = lax.axis_index("light"), sum(counts)
    for c, whole in enumerate(wholes):
        for i, k in enumerate(farthest_first(parts)):
            whole[z ^ k] = ins[c * parts + i][...]
    gram = jnp.zeros((parts * lights, parts * lights), f32)
    for r in range(wholes[0].shape[1] // counts[0]):
        page = [wholes[c][k, r * n : (r + 1) * n, :] for k in range(parts) for c, n in enumerate(counts)]
        page = jnp.concatenate(page, axis=0)
        gram += nt(page, page)
    gram *= scale
    for k in range(parts):
        blocks[k] = gram[k * lights : (k + 1) * lights]
    for k in range(parts):
        block = jnp.pad(blocks[z ^ k], ((0, 0), (0, view.shape[1] - parts * lights)))
        outs[k][...] = jnp.concatenate([block, view[...]], axis=0)


def place_kernel(counts, *refs):
    ins, core_ref = refs[:-1], refs[-1]
    v = lax.axis_index("view")
    ranks, width = core_ref.shape[0], ins[0].shape[1]
    for k in range(len(ins)):
        at = pl.ds(pl.multiple_of((v ^ k) * width, width), width)
        for r in range(ranks):
            begin, page = 0, []
            for n in counts:
                page.append(ins[k][begin + r * n : begin + (r + 1) * n, :])
                begin += ranks * n
            core_ref[r, :, at] = jnp.concatenate(page, axis=0)


def body(slab, basis):
    views, parts = lax.axis_size("view"), lax.axis_size("light")
    lights, rows, columns = slab.shape
    ranks = basis.shape[1]
    columns_all = columns * lax.axis_size("texel")
    view_scale = 1.0 / (lights * parts * columns_all)
    light_scale = 1.0 / (ranks * columns_all)
    width = columns // views
    views_all, lights_all = views * rows, parts * lights
    size = ranks // parts
    groups = max(g for g in range(1, width // ranks + 1) if rows % g == 0)
    head = -(-(rows // groups) // 16) * 16

    one = lights * 2 // 5 // 4 * 4
    counts, half = [one, lights - one], views // 2
    tall = [head + one * rows, (lights - one) * rows]

    blank = call(blank_kernel, sds((8, 128), f32), [], 10**9, [])

    spans = [(k, 0, lights if k < half else one) for k in range(views)]
    packed = call(
        functools.partial(pack_kernel, spans, groups, ranks, views),
        [sds((head + count * rows, width), bf16) for _, _, count in spans],
        [],
        0,
        [slab, basis],
        [blank],
    )
    came = swaps(packed, "view")
    near, whole = came[:half], [came[half:]]
    spans = [(k, one, lights - one) for k in range(half, views)]
    packed = call(
        functools.partial(pack_kernel, spans, 0, ranks, views),
        [sds((tall[1], width), bf16)] * len(spans),
        [],
        0,
        [slab],
        whole[0][1:],
    )
    moved = {k: swap(packed[k - half], "view", k) for k in farthest_first(views)[:half]}
    whole.append([moved[k] for k in range(half, views)])

    lit, carried, pieces = [], [], []
    for c, count in enumerate(counts):
        outs = [sds((size * count, width), bf16)] * parts + [sds((parts, size * count, width), bf16)]
        if c == 0:
            outs += [sds((ranks, views_all), bf16)]
        waits = lit[:1] if c else []
        made = call(
            functools.partial(
                core_kernel, count, 0 if c else head, [0] * half + [tall[0] * c] * half, rows, ranks, views, parts,
                0 if c else groups, len(waits),
            ),
            outs,
            [
                pltpu.VMEM((views, tall[c], width), bf16),
                pltpu.VMEM((width // 128, -(-count // 8) * 8 * ranks, 128), f32),
            ],
            2 * views_all * count * width * ranks,
            whole[c][::-1] + near[::-1] + carried,
            waits,
        )
        lit += swaps(made[:parts], "light")[::-1]
        pieces.append(made[parts])
        carried = list(made[parts + 1 :])
    back = call(
        functools.partial(back_kernel, 2), [sds((size * lights, width), bf16)] * views, [], 0, pieces, lit[: parts - 1]
    )
    spans = [(k, 0) for k in range(half)] + [(k, c * tall[0]) for c in range(2) for k in range(half, views)]
    wide = -(-max(3 * views_all // 2, lights_all) // 128) * 128
    view_part = call(
        functools.partial(view_kernel, lights, rows, views, spans, view_scale),
        sds((views_all // 2, wide), f32),
        [pltpu.VMEM((views, head + lights * rows, width), bf16)],
        2 * views_all * lights * width * views_all,
        near + whole[0] + whole[1],
    )
    returned = swaps(back, "view")
    sums = call(
        functools.partial(light_kernel, counts, 1, parts, light_scale),
        [sds((lights + views_all // 2, wide), f32)] * parts,
        [pltpu.VMEM((parts, size * count, width), bf16) for count in counts]
        + [pltpu.VMEM((parts, lights, lights_all), f32)],
        2 * lights_all * lights_all * size * width,
        lit + [view_part],
        [returned[1]],
    )
    dealt = call(
        functools.partial(deal_kernel, lights, rows, views),
        [sds((lights + rows, lights_all), f32)] * views,
        [pltpu.VMEM((views, rows, views_all), f32)],
        0,
        swaps(sums, "light")[::-1],
    )
    total = call(sum_kernel, sds((lights + rows, lights_all), f32), [], 0, swaps(dealt, "view")[::-1])
    total = doubled(total, "texel")
    core = call(
        functools.partial(place_kernel, counts),
        sds((ranks // views, lights, columns), bf16),
        [],
        0,
        returned,
    )
    return (total[lights:], core, total[:lights])


def solution(mesh):
    return jax.shard_map(
        body,
        mesh=mesh,
        in_specs=(P("light", "view", "texel"), P("view", None)),
        out_specs=(P("view", None), P("view", "light", "texel"), P("light", None)),
        check_vma=False,
    )
```

```python
import functools

import jax
import jax.numpy as jnp
from jax import lax
from jax.experimental import pallas as pl
from jax.experimental.pallas import tpu as pltpu
from jax.sharding import PartitionSpec as P

VMEM = pl.BlockSpec(memory_space=pltpu.VMEM)
ANY = pl.BlockSpec(memory_space=pl.ANY)
sds = jax.ShapeDtypeStruct
bf16, f32 = jnp.bfloat16, jnp.float32


def swap(value, axis, step):
    return lax.ppermute(value, axis, [(i, i ^ step) for i in range(lax.axis_size(axis))])


def farthest_first(n):
    return list(range(n - 1, -1, -1))


def swaps(values, axis):
    moved = {k: swap(values[k], axis, k) for k in farthest_first(len(values))[:-1]}
    return [values[0]] + [moved[k] for k in range(1, len(values))]


def summed(values):
    total = values[-1]
    for value in values[-2::-1]:
        total = total + value
    return total


def doubled(value, axis):
    step = 1
    while step < lax.axis_size(axis):
        value = value + swap(value, axis, step)
        step *= 2
    return value


def call(kernel, out_shape, scratch, flops, args, unused=()):
    moved = sum(a.size * a.dtype.itemsize for a in list(args) + jax.tree.leaves(out_shape))
    return pl.pallas_call(
        kernel,
        out_shape=out_shape,
        in_specs=[VMEM] * len(args) + [ANY] * len(unused),
        out_specs=jax.tree.map(lambda _: VMEM, out_shape),
        scratch_shapes=scratch,
        compiler_params=pltpu.CompilerParams(vmem_limit_bytes=32 * 1024 * 1024),
        cost_estimate=pl.CostEstimate(flops=flops, bytes_accessed=moved, transcendentals=0),
    )(*args, *unused)


def nt(a, b):
    return lax.dot_general(a, b, (((1,), (1,)), ((), ())), preferred_element_type=f32)


def cut(refs, *counts):
    out, at = [], 0
    for count in counts:
        out.append(refs[at : at + count])
        at += count
    return out + [refs[at:]]


def blank_kernel(out_ref):
    out_ref[...] = jnp.zeros_like(out_ref)


def pack_kernel(spans, groups, ranks, views, slab_ref, *refs):
    me = lax.axis_index("view")
    outs = refs[-len(spans) :]
    rows, columns = slab_ref.shape[1:]
    width = columns // views
    head = []
    if groups:
        deep = rows // groups
        wide = refs[0][...].astype(f32)
        wide = jnp.concatenate([wide[g * deep : (g + 1) * deep] for g in range(groups)], axis=1)
        head = [jnp.pad(wide, ((0, -deep % 16), (0, width - groups * ranks))).astype(bf16)]
    for (k, begin, count), out in zip(spans, outs):
        at = pl.ds(pl.multiple_of((me ^ k) * width, width), width)
        out[...] = jnp.concatenate(head + [slab_ref[l, :, at] for l in range(begin, begin + count)], axis=0)


def core_kernel(lights, head, starts, rows, ranks, views, parts, groups, spare, *refs):
    first = groups > 0
    ins, old, _, light_outs, (pieces, *outs) = cut(refs[:-2], views, 0 if first else 1, spare, parts)
    whole, turned = refs[-2:]
    v, z = lax.axis_index("view"), lax.axis_index("light")
    width = whole.shape[2]
    for i, k in enumerate(farthest_first(views)):
        whole[v ^ k] = ins[i][starts[i] : starts[i] + whole.shape[1], :]
    if first:
        deep = rows // groups
        wide = [whole[k, :head, :].astype(f32)[:deep] for k in range(views)]
        basis = jnp.concatenate([w[:, g * ranks : (g + 1) * ranks] for w in wide for g in range(groups)], axis=0)
        basis = jnp.pad(basis, ((0, 0), (0, 128 - ranks))).T[:ranks].astype(bf16)
    else:
        basis = old[0][...]
    for l in range(lights):
        at = head + l * rows
        page = jnp.concatenate([whole[k, at : at + rows, :] for k in range(views)], axis=0)
        product = jnp.dot(basis, page, preferred_element_type=f32)
        for h in range(width // 128):
            turned[h, l * ranks : (l + 1) * ranks, :] = product[:, h * 128 : (h + 1) * 128]
    size = ranks // parts
    for j in range(parts):
        for h in range(width // 128):
            picked = [turned[h, pl.ds(j * size + r, lights, stride=ranks), :] for r in range(size)]
            pieces[j, :, h * 128 : (h + 1) * 128] = jnp.concatenate(picked, axis=0).astype(bf16)
    for k in range(parts):
        light_outs[k][...] = pieces[z ^ k]
    if first:
        outs[0][...] = basis


def back_kernel(chunks, near, *refs):
    views = refs[0].shape[0]
    v, outs = lax.axis_index("view"), refs[-(views + near - 1) :]
    for k in range(views):
        page = jnp.concatenate([ref[v ^ k] for ref in refs[:chunks]], axis=0)
        outs[0][...] = page[: outs[0].shape[0]]
        if 0 < k < near:
            outs[1][...] = page[page.shape[0] - outs[1].shape[0] :]
        outs = outs[2 if 0 < k < near else 1 :]


def view_kernel(lights, rows, views, spans, scale, *refs):
    ins, (out, whole) = cut(refs, len(spans))
    v = lax.axis_index("view")
    for (k, begin), ref in zip(spans, ins):
        whole[v ^ k, begin : begin + ref.shape[0], :] = ref[...]
    head = whole.shape[1] - lights * rows
    gram = jnp.zeros((views * rows, views * rows), f32)
    for l in range(lights):
        at = head + l * rows
        page = jnp.concatenate([whole[k, at : at + rows, :] for k in range(views)], axis=0)
        gram += nt(page, page)
    gram *= scale
    half = views * rows // 2
    quarters = jnp.concatenate([gram[:half], gram[half:, half:]], axis=1)
    out[...] = jnp.pad(quarters, ((0, 0), (0, out.shape[1] - 3 * half)))


def deal_kernel(lights, rows, views, *refs):
    ins, outs, (blocks,) = cut(refs, len(refs) - views - 1, views)
    v = lax.axis_index("view")
    total = summed([ref[...] for ref in ins])
    light, quarters = total[:lights, : outs[0].shape[1]], total[lights:]
    half = views * rows // 2
    cross = quarters[:, half : 2 * half]
    lower = jnp.concatenate([cross.T, quarters[:, 2 * half : 3 * half]], axis=1)
    gram = jnp.concatenate([quarters[:, : 2 * half], lower], axis=0)
    for k in range(views):
        blocks[k] = gram[k * rows : (k + 1) * rows]
    for k in range(views):
        outs[k][...] = jnp.concatenate([light, blocks[v ^ k]], axis=0)


def sum_kernel(*refs):
    refs[-1][...] = summed([ref[...] for ref in refs[:-1]])


def light_kernel(counts, spare, parts, scale, *refs):
    ins, (view,), _, outs, wholes, (blocks,) = cut(refs, parts * len(counts), 1, spare, parts, len(counts))
    z, lights = lax.axis_index("light"), sum(counts)
    for c, whole in enumerate(wholes):
        for i, k in enumerate(farthest_first(parts)):
            whole[z ^ k] = ins[c * parts + i][...]
    gram = jnp.zeros((parts * lights, parts * lights), f32)
    for r in range(wholes[0].shape[1] // counts[0]):
        page = [wholes[c][k, r * n : (r + 1) * n, :] for k in range(parts) for c, n in enumerate(counts)]
        page = jnp.concatenate(page, axis=0)
        gram += nt(page, page)
    gram *= scale
    for k in range(parts):
        blocks[k] = gram[k * lights : (k + 1) * lights]
    for k in range(parts):
        block = jnp.pad(blocks[z ^ k], ((0, 0), (0, view.shape[1] - parts * lights)))
        outs[k][...] = jnp.concatenate([block, view[...]], axis=0)


def place_kernel(counts, halves, *refs):
    ins, core_ref = refs[:-1], refs[-1]
    v = lax.axis_index("view")
    ranks, width = core_ref.shape[0], ins[0].shape[1]
    tall = ranks * sum(counts)
    ins = [
        part[0] if len(part) == 1 else jnp.concatenate([part[0][...], part[1][2 * part[1].shape[0] - tall :]], axis=0)
        for part in cut(ins, *halves)[:-1]
    ]
    for k in range(len(ins)):
        at = pl.ds(pl.multiple_of((v ^ k) * width, width), width)
        for r in range(ranks):
            begin, page = 0, []
            for n in counts:
                page.append(ins[k][begin + r * n : begin + (r + 1) * n, :])
                begin += ranks * n
            core_ref[r, :, at] = jnp.concatenate(page, axis=0)


def body(slab, basis):
    views, parts = lax.axis_size("view"), lax.axis_size("light")
    lights, rows, columns = slab.shape
    ranks = basis.shape[1]
    columns_all = columns * lax.axis_size("texel")
    view_scale = 1.0 / (lights * parts * columns_all)
    light_scale = 1.0 / (ranks * columns_all)
    width = columns // views
    views_all, lights_all = views * rows, parts * lights
    size = ranks // parts
    groups = max(g for g in range(1, width // ranks + 1) if rows % g == 0)
    head = -(-(rows // groups) // 16) * 16

    one = lights * 2 // 5 // 4 * 4
    counts, half = [one, lights - one], views // 2
    tall = [head + one * rows, (lights - one) * rows]

    blank = call(blank_kernel, sds((8, 128), f32), [], 10**9, [])

    spans = [(k, 0, lights if k < half else one) for k in range(views)]
    packed = call(
        functools.partial(pack_kernel, spans, groups, ranks, views),
        [sds((head + count * rows, width), bf16) for _, _, count in spans],
        [],
        0,
        [slab, basis],
        [blank],
    )
    came = swaps(packed, "view")
    near, whole = came[:half], [came[half:]]
    spans = [(k, one, lights - one) for k in range(half, views)]
    packed = call(
        functools.partial(pack_kernel, spans, 0, ranks, views),
        [sds((tall[1], width), bf16)] * len(spans),
        [],
        0,
        [slab],
        whole[0][1:],
    )
    moved = {k: swap(packed[k - half], "view", k) for k in farthest_first(views)[:half]}
    whole.append([moved[k] for k in range(half, views)])

    lit, carried, pieces = [], [], []
    for c, count in enumerate(counts):
        outs = [sds((size * count, width), bf16)] * parts + [sds((parts, size * count, width), bf16)]
        if c == 0:
            outs += [sds((ranks, views_all), bf16)]
        waits = lit[:1] if c else []
        made = call(
            functools.partial(
                core_kernel, count, 0 if c else head, [0] * half + [tall[0] * c] * half, rows, ranks, views, parts,
                0 if c else groups, len(waits),
            ),
            outs,
            [
                pltpu.VMEM((views, tall[c], width), bf16),
                pltpu.VMEM((width // 128, -(-count // 8) * 8 * ranks, 128), f32),
            ],
            2 * views_all * count * width * ranks,
            whole[c][::-1] + near[::-1] + carried,
            waits,
        )
        lit += swaps(made[:parts], "light")[::-1]
        pieces.append(made[parts])
        carried = list(made[parts + 1 :])
    spans = [(k, 0) for k in range(half)] + [(k, c * tall[0]) for c in range(2) for k in range(half, views)]
    wide = -(-max(3 * views_all // 2, lights_all) // 128) * 128
    view_part = call(
        functools.partial(view_kernel, lights, rows, views, spans, view_scale),
        sds((views_all // 2, wide), f32),
        [pltpu.VMEM((views, head + lights * rows, width), bf16)],
        2 * views_all * lights * width * views_all,
        near + whole[0] + whole[1],
    )
    halves = [2 if 0 < k < half else 1 for k in range(views)]
    back = call(
        functools.partial(back_kernel, len(pieces), half),
        [sds((size * (counts[-1] if n > 1 else lights), width), bf16) for n in halves for _ in range(n)],
        [],
        0,
        pieces,
        lit[: parts - 1] + [view_part],
    )
    back = cut(back, *halves)[:-1]
    moved = {k: [swap(part, "view", k) for part in back[k]] for k in farthest_first(views)[:-1]}
    returned = [list(back[0])] + [moved[k] for k in range(1, views)]
    sums = call(
        functools.partial(light_kernel, counts, 2, parts, light_scale),
        [sds((lights + views_all // 2, wide), f32)] * parts,
        [pltpu.VMEM((parts, size * count, width), bf16) for count in counts]
        + [pltpu.VMEM((parts, lights, lights_all), f32)],
        2 * lights_all * lights_all * size * width,
        lit + [view_part],
        returned[1],
    )
    dealt = call(
        functools.partial(deal_kernel, lights, rows, views),
        [sds((lights + rows, lights_all), f32)] * views,
        [pltpu.VMEM((views, rows, views_all), f32)],
        0,
        swaps(sums, "light")[::-1],
    )
    total = call(sum_kernel, sds((lights + rows, lights_all), f32), [], 0, swaps(dealt, "view")[::-1])
    total = doubled(total, "texel")
    core = call(
        functools.partial(place_kernel, counts, halves),
        sds((ranks // views, lights, columns), bf16),
        [],
        0,
        sum(returned, []),
    )
    return (total[lights:], core, total[:lights])


def solution(mesh):
    return jax.shard_map(
        body,
        mesh=mesh,
        in_specs=(P("light", "view", "texel"), P("view", None)),
        out_specs=(P("view", None), P("view", "light", "texel"), P("light", None)),
        check_vma=False,
    )
```

```python
import functools

import jax
import jax.numpy as jnp
from jax import lax
from jax.experimental import pallas as pl
from jax.experimental.pallas import tpu as pltpu
from jax.sharding import PartitionSpec as P

VMEM = pl.BlockSpec(memory_space=pltpu.VMEM)
ANY = pl.BlockSpec(memory_space=pl.ANY)
sds = jax.ShapeDtypeStruct
bf16, f32 = jnp.bfloat16, jnp.float32


def swap(value, axis, step):
    return lax.ppermute(value, axis, [(i, i ^ step) for i in range(lax.axis_size(axis))])


def farthest_first(n):
    return list(range(n - 1, -1, -1))


def swaps(values, axis):
    moved = {k: swap(values[k], axis, k) for k in farthest_first(len(values))[:-1]}
    return [values[0]] + [moved[k] for k in range(1, len(values))]


def summed(values):
    total = values[-1]
    for value in values[-2::-1]:
        total = total + value
    return total


def doubled(value, axis):
    step = 1
    while step < lax.axis_size(axis):
        value = value + swap(value, axis, step)
        step *= 2
    return value


def call(kernel, out_shape, scratch, flops, args, unused=()):
    moved = sum(a.size * a.dtype.itemsize for a in list(args) + jax.tree.leaves(out_shape))
    return pl.pallas_call(
        kernel,
        out_shape=out_shape,
        in_specs=[VMEM] * len(args) + [ANY] * len(unused),
        out_specs=jax.tree.map(lambda _: VMEM, out_shape),
        scratch_shapes=scratch,
        compiler_params=pltpu.CompilerParams(vmem_limit_bytes=32 * 1024 * 1024),
        cost_estimate=pl.CostEstimate(flops=flops, bytes_accessed=moved, transcendentals=0),
    )(*args, *unused)


def nt(a, b):
    return lax.dot_general(a, b, (((1,), (1,)), ((), ())), preferred_element_type=f32)


def cut(refs, *counts):
    out, at = [], 0
    for count in counts:
        out.append(refs[at : at + count])
        at += count
    return out + [refs[at:]]


def blank_kernel(out_ref):
    out_ref[...] = jnp.zeros_like(out_ref)


def pack_kernel(spans, groups, ranks, views, slab_ref, *refs):
    me = lax.axis_index("view")
    outs = refs[-len(spans) :]
    rows, columns = slab_ref.shape[1:]
    width = columns // views
    head = []
    if groups:
        deep = rows // groups
        wide = refs[0][...].astype(f32)
        wide = jnp.concatenate([wide[g * deep : (g + 1) * deep] for g in range(groups)], axis=1)
        head = [jnp.pad(wide, ((0, -deep % 16), (0, width - groups * ranks))).astype(bf16)]
    for (k, begin, count), out in zip(spans, outs):
        at = pl.ds(pl.multiple_of((me ^ k) * width, width), width)
        out[...] = jnp.concatenate(head + [slab_ref[l, :, at] for l in range(begin, begin + count)], axis=0)


def core_kernel(lights, head, starts, rows, ranks, views, parts, groups, spare, *refs):
    first = groups > 0
    ins, old, _, light_outs, (pieces, *outs) = cut(refs[:-2], views, 0 if first else 1, spare, parts)
    whole, turned = refs[-2:]
    v, z = lax.axis_index("view"), lax.axis_index("light")
    width = whole.shape[2]
    for i, k in enumerate(farthest_first(views)):
        whole[v ^ k] = ins[i][starts[i] : starts[i] + whole.shape[1], :]
    if first:
        deep = rows // groups
        wide = [whole[k, :head, :].astype(f32)[:deep] for k in range(views)]
        basis = jnp.concatenate([w[:, g * ranks : (g + 1) * ranks] for w in wide for g in range(groups)], axis=0)
        basis = jnp.pad(basis, ((0, 0), (0, 128 - ranks))).T[:ranks].astype(bf16)
    else:
        basis = old[0][...]
    for l in range(lights):
        at = head + l * rows
        page = jnp.concatenate([whole[k, at : at + rows, :] for k in range(views)], axis=0)
        product = jnp.dot(basis, page, preferred_element_type=f32)
        for h in range(width // 128):
            turned[h, l * ranks : (l + 1) * ranks, :] = product[:, h * 128 : (h + 1) * 128]
    size = ranks // parts
    for j in range(parts):
        for h in range(width // 128):
            picked = [turned[h, pl.ds(j * size + r, lights, stride=ranks), :] for r in range(size)]
            pieces[j, :, h * 128 : (h + 1) * 128] = jnp.concatenate(picked, axis=0).astype(bf16)
    for k in range(parts):
        light_outs[k][...] = pieces[z ^ k]
    if first:
        outs[0][...] = basis


def back_kernel(chunks, *refs):
    v, outs = lax.axis_index("view"), refs[-refs[0].shape[0] :]
    for k, out in enumerate(outs):
        out[...] = jnp.concatenate([ref[v ^ k] for ref in refs[:chunks]], axis=0)


def view_kernel(lights, rows, views, spans, scale, *refs):
    ins, (out, whole) = cut(refs, len(spans))
    v = lax.axis_index("view")
    for (k, begin), ref in zip(spans, ins):
        whole[v ^ k, begin : begin + ref.shape[0], :] = ref[...]
    head = whole.shape[1] - lights * rows
    gram = jnp.zeros((views * rows, views * rows), f32)
    for l in range(lights):
        at = head + l * rows
        page = jnp.concatenate([whole[k, at : at + rows, :] for k in range(views)], axis=0)
        gram += nt(page, page)
    gram *= scale
    half = views * rows // 2
    quarters = jnp.concatenate([gram[:half], gram[half:, half:]], axis=1)
    out[...] = jnp.pad(quarters, ((0, 0), (0, out.shape[1] - 3 * half)))


def deal_kernel(lights, rows, views, *refs):
    ins, outs, (blocks,) = cut(refs, len(refs) - views - 1, views)
    v = lax.axis_index("view")
    total = summed([ref[...] for ref in ins])
    light, quarters = total[:lights, : outs[0].shape[1]], total[lights:]
    half = views * rows // 2
    cross = quarters[:, half : 2 * half]
    lower = jnp.concatenate([cross.T, quarters[:, 2 * half : 3 * half]], axis=1)
    gram = jnp.concatenate([quarters[:, : 2 * half], lower], axis=0)
    for k in range(views):
        blocks[k] = gram[k * rows : (k + 1) * rows]
    for k in range(views):
        outs[k][...] = jnp.concatenate([light, blocks[v ^ k]], axis=0)


def sum_kernel(*refs):
    refs[-1][...] = summed([ref[...] for ref in refs[:-1]])


def light_kernel(counts, spare, parts, scale, *refs):
    ins, (view,), _, outs, wholes, (blocks,) = cut(refs, parts * len(counts), 1, spare, parts, len(counts))
    z, lights = lax.axis_index("light"), sum(counts)
    for c, whole in enumerate(wholes):
        for i, k in enumerate(farthest_first(parts)):
            whole[z ^ k] = ins[c * parts + i][...]
    gram = jnp.zeros((parts * lights, parts * lights), f32)
    for r in range(wholes[0].shape[1] // counts[0]):
        page = [wholes[c][k, r * n : (r + 1) * n, :] for k in range(parts) for c, n in enumerate(counts)]
        page = jnp.concatenate(page, axis=0)
        gram += nt(page, page)
    gram *= scale
    for k in range(parts):
        blocks[k] = gram[k * lights : (k + 1) * lights]
    for k in range(parts):
        block = jnp.pad(blocks[z ^ k], ((0, 0), (0, view.shape[1] - parts * lights)))
        outs[k][...] = jnp.concatenate([block, view[...]], axis=0)


def place_kernel(counts, *refs):
    ins, core_ref = refs[:-1], refs[-1]
    v = lax.axis_index("view")
    ranks, width = core_ref.shape[0], ins[0].shape[1]
    for k in range(len(ins)):
        at = pl.ds(pl.multiple_of((v ^ k) * width, width), width)
        for r in range(ranks):
            begin, page = 0, []
            for n in counts:
                page.append(ins[k][begin + r * n : begin + (r + 1) * n, :])
                begin += ranks * n
            core_ref[r, :, at] = jnp.concatenate(page, axis=0)


def body(slab, basis):
    views, parts = lax.axis_size("view"), lax.axis_size("light")
    lights, rows, columns = slab.shape
    ranks = basis.shape[1]
    columns_all = columns * lax.axis_size("texel")
    view_scale = 1.0 / (lights * parts * columns_all)
    light_scale = 1.0 / (ranks * columns_all)
    width = columns // views
    views_all, lights_all = views * rows, parts * lights
    size = ranks // parts
    groups = max(g for g in range(1, width // ranks + 1) if rows % g == 0)
    head = -(-(rows // groups) // 16) * 16

    one = lights * 2 // 5 // 4 * 4
    counts, half = [one, lights - one], views // 2
    tall = [head + one * rows, (lights - one) * rows]

    blank = call(blank_kernel, sds((8, 128), f32), [], 10**9, [])

    spans = [(k, 0, lights if k < half else one) for k in range(views)]
    packed = call(
        functools.partial(pack_kernel, spans, groups, ranks, views),
        [sds((head + count * rows, width), bf16) for _, _, count in spans],
        [],
        0,
        [slab, basis],
        [blank],
    )
    came = swaps(packed, "view")
    near, whole = came[:half], [came[half:]]
    spans = [(k, one, lights - one) for k in range(half, views)]
    packed = call(
        functools.partial(pack_kernel, spans, 0, ranks, views),
        [sds((tall[1], width), bf16)] * len(spans),
        [],
        0,
        [slab],
        near[1:],
    )
    moved = {k: swap(packed[k - half], "view", k) for k in farthest_first(views)[:half]}
    whole.append([moved[k] for k in range(half, views)])

    lit, carried, pieces = [], [], []
    for c, count in enumerate(counts):
        outs = [sds((size * count, width), bf16)] * parts + [sds((parts, size * count, width), bf16)]
        if c == 0:
            outs += [sds((ranks, views_all), bf16)]
        waits = lit[:1] if c else []
        made = call(
            functools.partial(
                core_kernel, count, 0 if c else head, [0] * half + [tall[0] * c] * half, rows, ranks, views, parts,
                0 if c else groups, len(waits),
            ),
            outs,
            [
                pltpu.VMEM((views, tall[c], width), bf16),
                pltpu.VMEM((width // 128, -(-count // 8) * 8 * ranks, 128), f32),
            ],
            2 * views_all * count * width * ranks,
            whole[c][::-1] + near[::-1] + carried,
            waits,
        )
        lit += swaps(made[:parts], "light")[::-1]
        pieces.append(made[parts])
        carried = list(made[parts + 1 :])
    back = call(
        functools.partial(back_kernel, 2), [sds((size * lights, width), bf16)] * views, [], 0, pieces, lit[: parts - 1]
    )
    spans = [(k, 0) for k in range(half)] + [(k, c * tall[0]) for c in range(2) for k in range(half, views)]
    wide = -(-max(3 * views_all // 2, lights_all) // 128) * 128
    view_part = call(
        functools.partial(view_kernel, lights, rows, views, spans, view_scale),
        sds((views_all // 2, wide), f32),
        [pltpu.VMEM((views, head + lights * rows, width), bf16)],
        2 * views_all * lights * width * views_all,
        near + whole[0] + whole[1],
    )
    returned = swaps(back, "view")
    sums = call(
        functools.partial(light_kernel, counts, 1, parts, light_scale),
        [sds((lights + views_all // 2, wide), f32)] * parts,
        [pltpu.VMEM((parts, size * count, width), bf16) for count in counts]
        + [pltpu.VMEM((parts, lights, lights_all), f32)],
        2 * lights_all * lights_all * size * width,
        lit + [view_part],
        [returned[1]],
    )
    dealt = call(
        functools.partial(deal_kernel, lights, rows, views),
        [sds((lights + rows, lights_all), f32)] * views,
        [pltpu.VMEM((views, rows, views_all), f32)],
        0,
        swaps(sums, "light")[::-1],
    )
    total = call(sum_kernel, sds((lights + rows, lights_all), f32), [], 0, swaps(dealt, "view")[::-1])
    total = doubled(total, "texel")
    core = call(
        functools.partial(place_kernel, counts),
        sds((ranks // views, lights, columns), bf16),
        [],
        0,
        returned,
    )
    return (total[lights:], core, total[:lights])


def solution(mesh):
    return jax.shard_map(
        body,
        mesh=mesh,
        in_specs=(P("light", "view", "texel"), P("view", None)),
        out_specs=(P("view", None), P("view", "light", "texel"), P("light", None)),
        check_vma=False,
    )
```

```python
import functools

import jax
import jax.numpy as jnp
from jax import lax
from jax.experimental import pallas as pl
from jax.experimental.pallas import tpu as pltpu
from jax.sharding import PartitionSpec as P

VMEM = pl.BlockSpec(memory_space=pltpu.VMEM)
ANY = pl.BlockSpec(memory_space=pl.ANY)
sds = jax.ShapeDtypeStruct
bf16, f32 = jnp.bfloat16, jnp.float32


def swap(value, axis, step):
    return lax.ppermute(value, axis, [(i, i ^ step) for i in range(lax.axis_size(axis))])


def farthest_first(n):
    return list(range(n - 1, -1, -1))


def swaps(values, axis):
    moved = {k: swap(values[k], axis, k) for k in farthest_first(len(values))[:-1]}
    return [values[0]] + [moved[k] for k in range(1, len(values))]


def summed(values):
    total = values[-1]
    for value in values[-2::-1]:
        total = total + value
    return total


def call(kernel, out_shape, scratch, flops, args, unused=()):
    moved = sum(a.size * a.dtype.itemsize for a in list(args) + jax.tree.leaves(out_shape))
    return pl.pallas_call(
        kernel,
        out_shape=out_shape,
        in_specs=[VMEM] * len(args) + [ANY] * len(unused),
        out_specs=jax.tree.map(lambda _: VMEM, out_shape),
        scratch_shapes=scratch,
        compiler_params=pltpu.CompilerParams(vmem_limit_bytes=32 * 1024 * 1024),
        cost_estimate=pl.CostEstimate(flops=flops, bytes_accessed=moved, transcendentals=0),
    )(*args, *unused)


def nt(a, b):
    return lax.dot_general(a, b, (((1,), (1,)), ((), ())), preferred_element_type=f32)


def cut(refs, *counts):
    out, at = [], 0
    for count in counts:
        out.append(refs[at : at + count])
        at += count
    return out + [refs[at:]]


def blank_kernel(out_ref):
    out_ref[...] = jnp.zeros_like(out_ref)


def pack_kernel(spans, groups, ranks, views, slab_ref, *refs):
    me = lax.axis_index("view")
    outs = refs[-len(spans) :]
    rows, columns = slab_ref.shape[1:]
    width = columns // views
    head = []
    if groups:
        deep = rows // groups
        wide = refs[0][...].astype(f32)
        wide = jnp.concatenate([wide[g * deep : (g + 1) * deep] for g in range(groups)], axis=1)
        head = [jnp.pad(wide, ((0, -deep % 16), (0, width - groups * ranks))).astype(bf16)]
    for (k, begin, count), out in zip(spans, outs):
        at = pl.ds(pl.multiple_of((me ^ k) * width, width), width)
        out[...] = jnp.concatenate(head + [slab_ref[l, :, at] for l in range(begin, begin + count)], axis=0)


def core_kernel(lights, head, starts, rows, ranks, views, parts, groups, spare, *refs):
    first = groups > 0
    ins, old, _, light_outs, (pieces, *outs) = cut(refs[:-2], views, 0 if first else 1, spare, parts)
    whole, turned = refs[-2:]
    v, z = lax.axis_index("view"), lax.axis_index("light")
    width = whole.shape[2]
    for i, k in enumerate(farthest_first(views)):
        whole[v ^ k] = ins[i][starts[i] : starts[i] + whole.shape[1], :]
    if first:
        deep = rows // groups
        wide = [whole[k, :head, :].astype(f32)[:deep] for k in range(views)]
        basis = jnp.concatenate([w[:, g * ranks : (g + 1) * ranks] for w in wide for g in range(groups)], axis=0)
        basis = jnp.pad(basis, ((0, 0), (0, 128 - ranks))).T[:ranks].astype(bf16)
    else:
        basis = old[0][...]
    for l in range(lights):
        at = head + l * rows
        page = jnp.concatenate([whole[k, at : at + rows, :] for k in range(views)], axis=0)
        product = jnp.dot(basis, page, preferred_element_type=f32)
        for h in range(width // 128):
            turned[h, l * ranks : (l + 1) * ranks, :] = product[:, h * 128 : (h + 1) * 128]
    size = ranks // parts
    for j in range(parts):
        for h in range(width // 128):
            picked = [turned[h, pl.ds(j * size + r, lights, stride=ranks), :] for r in range(size)]
            pieces[j, :, h * 128 : (h + 1) * 128] = jnp.concatenate(picked, axis=0).astype(bf16)
    for k in range(parts):
        light_outs[k][...] = pieces[z ^ k]
    if first:
        outs[0][...] = basis


def back_kernel(chunks, *refs):
    v, outs = lax.axis_index("view"), refs[-refs[0].shape[0] :]
    for k, out in enumerate(outs):
        out[...] = jnp.concatenate([ref[v ^ k] for ref in refs[:chunks]], axis=0)


def view_kernel(lights, rows, views, spans, scale, *refs):
    ins, (out, whole) = cut(refs, len(spans))
    v = lax.axis_index("view")
    for (k, begin), ref in zip(spans, ins):
        whole[v ^ k, begin : begin + ref.shape[0], :] = ref[...]
    head = whole.shape[1] - lights * rows
    gram = jnp.zeros((views * rows, views * rows), f32)
    for l in range(lights):
        at = head + l * rows
        page = jnp.concatenate([whole[k, at : at + rows, :] for k in range(views)], axis=0)
        gram += nt(page, page)
    gram *= scale
    half = views * rows // 2
    left = jnp.zeros((out.shape[1], out.shape[2] - half), f32)
    for p in range(2):
        mine = jnp.concatenate([gram[k * rows : (k + 1) * rows] for k in range(p, views, 2)], axis=0)
        mine = jnp.concatenate([mine[:, :half], mine[:, half:]], axis=0)
        out[p] = jnp.concatenate([left, mine], axis=1)


def deal_light_kernel(lights, parts, keep_ref, came_ref, *refs):
    outs, blocks = refs[:-1], refs[-1]
    z = lax.axis_index("light")
    total = keep_ref[...] + came_ref[...]
    wide = lights * parts
    tall = total.shape[0] // 2
    view = total[:, total.shape[1] - tall :]
    view = jnp.concatenate([view[:tall], view[tall:]], axis=1)
    for k in range(parts):
        light = total[k * lights : (k + 1) * lights, :wide]
        light = jnp.concatenate([light[:, : wide // 2], light[:, wide // 2 :]], axis=0)
        blocks[k] = jnp.concatenate([view, light], axis=1)
    for k in range(parts):
        outs[k][...] = blocks[z ^ k]


def deal_view_kernel(lights, rows, spare, *refs):
    total_ref, outs, blocks = refs[0], refs[1 + spare : -1], refs[-1]
    u = lax.axis_index("view") // 2
    total = total_ref[...]
    wide = 2 * rows * len(outs)
    light = total[:, wide:]
    light = jnp.concatenate([light[:lights], light[lights:]], axis=1)
    for m in range(len(outs)):
        blocks[m] = jnp.concatenate([light, total[m * rows : (m + 1) * rows, :wide]], axis=0)
    for m in range(len(outs)):
        outs[m][...] = blocks[u ^ m]


def sum_kernel(*refs):
    refs[-1][...] = summed([ref[...] for ref in refs[:-1]])


def light_kernel(counts, spare, parts, scale, *refs):
    ins, (view,), _, (keep_out, send_out), wholes = cut(refs, parts * len(counts), 1, spare, 2)
    z, lights = lax.axis_index("light"), sum(counts)
    for c, whole in enumerate(wholes):
        for i, k in enumerate(farthest_first(parts)):
            whole[z ^ k] = ins[c * parts + i][...]
    gram = jnp.zeros((parts * lights, parts * lights), f32)
    for r in range(wholes[0].shape[1] // counts[0]):
        page = [wholes[c][k, r * n : (r + 1) * n, :] for k in range(parts) for c, n in enumerate(counts)]
        page = jnp.concatenate(page, axis=0)
        gram += nt(page, page)
    gram *= scale
    gram = jnp.pad(gram, ((0, keep_out.shape[0] - gram.shape[0]), (0, keep_out.shape[1] - gram.shape[1])))
    parity = lax.axis_index("view") % 2
    keep_out[...] = gram + view[parity]
    send_out[...] = gram + view[1 - parity]


def place_kernel(counts, *refs):
    ins, core_ref = refs[:-1], refs[-1]
    v = lax.axis_index("view")
    ranks, width = core_ref.shape[0], ins[0].shape[1]
    for k in range(len(ins)):
        at = pl.ds(pl.multiple_of((v ^ k) * width, width), width)
        for r in range(ranks):
            begin, page = 0, []
            for n in counts:
                page.append(ins[k][begin + r * n : begin + (r + 1) * n, :])
                begin += ranks * n
            core_ref[r, :, at] = jnp.concatenate(page, axis=0)


def body(slab, basis):
    views, parts = lax.axis_size("view"), lax.axis_size("light")
    lights, rows, columns = slab.shape
    ranks = basis.shape[1]
    columns_all = columns * lax.axis_size("texel")
    view_scale = 1.0 / (lights * parts * columns_all)
    light_scale = 1.0 / (ranks * columns_all)
    width = columns // views
    views_all, lights_all = views * rows, parts * lights
    size = ranks // parts
    groups = max(g for g in range(1, width // ranks + 1) if rows % g == 0)
    head = -(-(rows // groups) // 16) * 16

    one = lights * 2 // 5 // 4 * 4
    counts, half = [one, lights - one], views // 2
    tall = [head + one * rows, (lights - one) * rows]

    blank = call(blank_kernel, sds((8, 128), f32), [], 10**9, [])

    spans = [(k, 0, lights if k < half else one) for k in range(views)]
    packed = call(
        functools.partial(pack_kernel, spans, groups, ranks, views),
        [sds((head + count * rows, width), bf16) for _, _, count in spans],
        [],
        0,
        [slab, basis],
        [blank],
    )
    came = swaps(packed, "view")
    near, whole = came[:half], [came[half:]]
    spans = [(k, one, lights - one) for k in range(half, views)]
    packed = call(
        functools.partial(pack_kernel, spans, 0, ranks, views),
        [sds((tall[1], width), bf16)] * len(spans),
        [],
        0,
        [slab],
        whole[0][1:],
    )
    moved = {k: swap(packed[k - half], "view", k) for k in farthest_first(views)[:half]}
    whole.append([moved[k] for k in range(half, views)])

    lit, carried, pieces = [], [], []
    for c, count in enumerate(counts):
        outs = [sds((size * count, width), bf16)] * parts + [sds((parts, size * count, width), bf16)]
        if c == 0:
            outs += [sds((ranks, views_all), bf16)]
        waits = lit[:1] if c else []
        made = call(
            functools.partial(
                core_kernel, count, 0 if c else head, [0] * half + [tall[0] * c] * half, rows, ranks, views, parts,
                0 if c else groups, len(waits),
            ),
            outs,
            [
                pltpu.VMEM((views, tall[c], width), bf16),
                pltpu.VMEM((width // 128, -(-count // 8) * 8 * ranks, 128), f32),
            ],
            2 * views_all * count * width * ranks,
            whole[c][::-1] + near[::-1] + carried,
            waits,
        )
        lit += swaps(made[:parts], "light")[::-1]
        pieces.append(made[parts])
        carried = list(made[parts + 1 :])
    back = call(
        functools.partial(back_kernel, 2), [sds((size * lights, width), bf16)] * views, [], 0, pieces, lit[: parts - 1]
    )
    spans = [(k, 0) for k in range(half)] + [(k, c * tall[0]) for c in range(2) for k in range(half, views)]
    wide = lights_all + views_all // 2
    both = max(lights_all, views_all)
    view_part = call(
        functools.partial(view_kernel, lights, rows, views, spans, view_scale),
        sds((2, both, wide), f32),
        [pltpu.VMEM((views, head + lights * rows, width), bf16)],
        2 * views_all * lights * width * views_all,
        near + whole[0] + whole[1],
    )
    returned = swaps(back, "view")
    keep, send = call(
        functools.partial(light_kernel, counts, 1, parts, light_scale),
        [sds((both, wide), f32)] * 2,
        [pltpu.VMEM((parts, size * count, width), bf16) for count in counts],
        2 * lights_all * lights_all * size * width,
        lit + [view_part],
        [returned[1]],
    )
    dealt = call(
        functools.partial(deal_light_kernel, lights, parts),
        [sds((views_all // 2, views_all + lights_all // 2), f32)] * parts,
        [pltpu.VMEM((parts, views_all // 2, views_all + lights_all // 2), f32)],
        0,
        [keep, swap(send, "view", 1)],
    )
    total = call(sum_kernel, sds(dealt[0].shape, f32), [], 0, swaps(dealt, "light")[::-1])
    texels, step = lax.axis_size("texel"), 2
    while step < texels:
        total = total + swap(total, "texel", step)
        step *= 2
    dealt = call(
        functools.partial(deal_view_kernel, lights, rows, 2),
        [sds((lights + rows, views_all), f32)] * half,
        [pltpu.VMEM((half, lights + rows, views_all), f32)],
        0,
        [total],
        [returned[2], returned[3]],
    )
    steps = [(t, m) for t in range(min(2, texels) - 1, -1, -1) for m in range(half - 1, -1, -1)]
    came = [swap(dealt[m], ("texel", "view"), t * views + 2 * m) for t, m in steps[:-1]]
    total = summed([dealt[0]] + came[::-1])
    core = call(
        functools.partial(place_kernel, counts),
        sds((ranks // views, lights, columns), bf16),
        [],
        0,
        returned,
    )
    return (total[lights:], core, total[:lights])


def solution(mesh):
    return jax.shard_map(
        body,
        mesh=mesh,
        in_specs=(P("light", "view", "texel"), P("view", None)),
        out_specs=(P("view", None), P("view", "light", "texel"), P("light", None)),
        check_vma=False,
    )
```

```python
import functools

import jax
import jax.numpy as jnp
from jax import lax
from jax.experimental import pallas as pl
from jax.experimental.pallas import tpu as pltpu
from jax.sharding import PartitionSpec as P

VMEM = pl.BlockSpec(memory_space=pltpu.VMEM)
ANY = pl.BlockSpec(memory_space=pl.ANY)
sds = jax.ShapeDtypeStruct
bf16, f32 = jnp.bfloat16, jnp.float32


def swap(value, axis, step):
    return lax.ppermute(value, axis, [(i, i ^ step) for i in range(lax.axis_size(axis))])


def farthest_first(n):
    return list(range(n - 1, -1, -1))


def swaps(values, axis):
    moved = {k: swap(values[k], axis, k) for k in farthest_first(len(values))[:-1]}
    return [values[0]] + [moved[k] for k in range(1, len(values))]


def summed(values):
    total = values[-1]
    for value in values[-2::-1]:
        total = total + value
    return total


def call(kernel, out_shape, scratch, flops, args, unused=()):
    moved = sum(a.size * a.dtype.itemsize for a in list(args) + jax.tree.leaves(out_shape))
    return pl.pallas_call(
        kernel,
        out_shape=out_shape,
        in_specs=[VMEM] * len(args) + [ANY] * len(unused),
        out_specs=jax.tree.map(lambda _: VMEM, out_shape),
        scratch_shapes=scratch,
        compiler_params=pltpu.CompilerParams(vmem_limit_bytes=32 * 1024 * 1024),
        cost_estimate=pl.CostEstimate(flops=flops, bytes_accessed=moved, transcendentals=0),
    )(*args, *unused)


def nt(a, b):
    return lax.dot_general(a, b, (((1,), (1,)), ((), ())), preferred_element_type=f32)


def cut(refs, *counts):
    out, at = [], 0
    for count in counts:
        out.append(refs[at : at + count])
        at += count
    return out + [refs[at:]]


def blank_kernel(out_ref):
    out_ref[...] = jnp.zeros_like(out_ref)


def pack_kernel(spans, groups, ranks, views, slab_ref, *refs):
    me = lax.axis_index("view")
    outs = refs[-len(spans) :]
    rows, columns = slab_ref.shape[1:]
    width = columns // views
    head = []
    if groups:
        deep = rows // groups
        wide = refs[0][...].astype(f32)
        wide = jnp.concatenate([wide[g * deep : (g + 1) * deep] for g in range(groups)], axis=1)
        head = [jnp.pad(wide, ((0, -deep % 16), (0, width - groups * ranks))).astype(bf16)]
    for (k, begin, count), out in zip(spans, outs):
        at = pl.ds(pl.multiple_of((me ^ k) * width, width), width)
        out[...] = jnp.concatenate(head + [slab_ref[l, :, at] for l in range(begin, begin + count)], axis=0)


def core_kernel(lights, head, starts, rows, ranks, views, parts, groups, spare, *refs):
    first = groups > 0
    ins, old, _, light_outs, (pieces, *outs) = cut(refs[:-2], views, 0 if first else 1, spare, parts)
    whole, turned = refs[-2:]
    v, z = lax.axis_index("view"), lax.axis_index("light")
    width = whole.shape[2]
    for i, k in enumerate(farthest_first(views)):
        whole[v ^ k] = ins[i][starts[i] : starts[i] + whole.shape[1], :]
    if first:
        deep = rows // groups
        wide = [whole[k, :head, :].astype(f32)[:deep] for k in range(views)]
        basis = jnp.concatenate([w[:, g * ranks : (g + 1) * ranks] for w in wide for g in range(groups)], axis=0)
        basis = jnp.pad(basis, ((0, 0), (0, 128 - ranks))).T[:ranks].astype(bf16)
    else:
        basis = old[0][...]
    for l in range(lights):
        at = head + l * rows
        page = jnp.concatenate([whole[k, at : at + rows, :] for k in range(views)], axis=0)
        product = jnp.dot(basis, page, preferred_element_type=f32)
        for h in range(width // 128):
            turned[h, l * ranks : (l + 1) * ranks, :] = product[:, h * 128 : (h + 1) * 128]
    size = ranks // parts
    for j in range(parts):
        for h in range(width // 128):
            picked = [turned[h, pl.ds(j * size + r, lights, stride=ranks), :] for r in range(size)]
            pieces[j, :, h * 128 : (h + 1) * 128] = jnp.concatenate(picked, axis=0).astype(bf16)
    for k in range(parts):
        light_outs[k][...] = pieces[z ^ k]
    if first:
        outs[0][...] = basis


def back_kernel(chunks, *refs):
    v, outs = lax.axis_index("view"), refs[-refs[0].shape[0] :]
    for k, out in enumerate(outs):
        out[...] = jnp.concatenate([ref[v ^ k] for ref in refs[:chunks]], axis=0)


def view_kernel(lights, rows, views, spans, scale, *refs):
    ins, (out, whole) = cut(refs, len(spans))
    v = lax.axis_index("view")
    for (k, begin), ref in zip(spans, ins):
        whole[v ^ k, begin : begin + ref.shape[0], :] = ref[...]
    head = whole.shape[1] - lights * rows
    gram = jnp.zeros((views * rows, views * rows), f32)
    for l in range(lights):
        at = head + l * rows
        page = jnp.concatenate([whole[k, at : at + rows, :] for k in range(views)], axis=0)
        gram += nt(page, page)
    gram *= scale
    half = views * rows // 2
    left = jnp.zeros((out.shape[1], out.shape[2] - half), f32)
    for p in range(2):
        mine = jnp.concatenate([gram[k * rows : (k + 1) * rows] for k in range(p, views, 2)], axis=0)
        mine = jnp.concatenate([mine[:, :half], mine[:, half:]], axis=0)
        out[p] = jnp.concatenate([left, mine], axis=1)


def deal_light_kernel(lights, parts, keep_ref, came_ref, *refs):
    outs, blocks = refs[:-1], refs[-1]
    z = lax.axis_index("light")
    total = keep_ref[...] + came_ref[...]
    wide = lights * parts
    tall = total.shape[0] // 2
    view = total[:, total.shape[1] - tall :]
    view = jnp.concatenate([view[:tall], view[tall:]], axis=1)
    for k in range(parts):
        light = total[k * lights : (k + 1) * lights, :wide]
        light = jnp.concatenate([light[:, : wide // 2], light[:, wide // 2 :]], axis=0)
        blocks[k] = jnp.concatenate([view, light], axis=1)
    for k in range(parts):
        outs[k][...] = blocks[z ^ k]


def deal_view_kernel(lights, rows, spare, *refs):
    total_ref, outs, blocks = refs[0], refs[1 + spare : -1], refs[-1]
    u = lax.axis_index("view") // 2
    total = total_ref[...]
    wide = 2 * rows * len(outs)
    light = total[:, wide:]
    light = jnp.concatenate([light[:lights], light[lights:]], axis=1)
    for m in range(len(outs)):
        blocks[m] = jnp.concatenate([light, total[m * rows : (m + 1) * rows, :wide]], axis=0)
    for m in range(len(outs)):
        outs[m][...] = blocks[u ^ m]


def sum_kernel(*refs):
    refs[-1][...] = summed([ref[...] for ref in refs[:-1]])


def light_kernel(counts, spare, parts, scale, *refs):
    ins, (view,), _, (keep_out, send_out), wholes = cut(refs, parts * len(counts), 1, spare, 2)
    z, lights = lax.axis_index("light"), sum(counts)
    for c, whole in enumerate(wholes):
        for i, k in enumerate(farthest_first(parts)):
            whole[z ^ k] = ins[c * parts + i][...]
    gram = jnp.zeros((parts * lights, parts * lights), f32)
    for r in range(wholes[0].shape[1] // counts[0]):
        page = [wholes[c][k, r * n : (r + 1) * n, :] for k in range(parts) for c, n in enumerate(counts)]
        page = jnp.concatenate(page, axis=0)
        gram += nt(page, page)
    gram *= scale
    gram = jnp.pad(gram, ((0, keep_out.shape[0] - gram.shape[0]), (0, keep_out.shape[1] - gram.shape[1])))
    parity = lax.axis_index("view") % 2
    keep_out[...] = gram + view[parity]
    send_out[...] = gram + view[1 - parity]


def place_kernel(counts, *refs):
    ins, core_ref = refs[:-1], refs[-1]
    v = lax.axis_index("view")
    ranks, width = core_ref.shape[0], ins[0].shape[1]
    for k in range(len(ins)):
        at = pl.ds(pl.multiple_of((v ^ k) * width, width), width)
        for r in range(ranks):
            begin, page = 0, []
            for n in counts:
                page.append(ins[k][begin + r * n : begin + (r + 1) * n, :])
                begin += ranks * n
            core_ref[r, :, at] = jnp.concatenate(page, axis=0)


def body(slab, basis):
    views, parts = lax.axis_size("view"), lax.axis_size("light")
    lights, rows, columns = slab.shape
    ranks = basis.shape[1]
    columns_all = columns * lax.axis_size("texel")
    view_scale = 1.0 / (lights * parts * columns_all)
    light_scale = 1.0 / (ranks * columns_all)
    width = columns // views
    views_all, lights_all = views * rows, parts * lights
    size = ranks // parts
    groups = max(g for g in range(1, width // ranks + 1) if rows % g == 0)
    head = -(-(rows // groups) // 16) * 16

    one = lights * 2 // 5 // 4 * 4
    counts, half = [one, lights - one], views // 2
    tall = [head + one * rows, (lights - one) * rows]

    blank = call(blank_kernel, sds((8, 128), f32), [], 10**9, [])

    spans = [(k, 0, lights if k < half else one) for k in range(views)]
    packed = call(
        functools.partial(pack_kernel, spans, groups, ranks, views),
        [sds((head + count * rows, width), bf16) for _, _, count in spans],
        [],
        0,
        [slab, basis],
        [blank],
    )
    came = swaps(packed, "view")
    near, whole = came[:half], [came[half:]]
    spans = [(k, one, lights - one) for k in range(half, views)]
    packed = call(
        functools.partial(pack_kernel, spans, 0, ranks, views),
        [sds((tall[1], width), bf16)] * len(spans),
        [],
        0,
        [slab],
        whole[0][1:],
    )
    moved = {k: swap(packed[k - half], "view", k) for k in farthest_first(views)[:half]}
    whole.append([moved[k] for k in range(half, views)])

    lit, carried, pieces = [], [], []
    for c, count in enumerate(counts):
        outs = [sds((size * count, width), bf16)] * parts + [sds((parts, size * count, width), bf16)]
        if c == 0:
            outs += [sds((ranks, views_all), bf16)]
        waits = lit[:1] if c else []
        made = call(
            functools.partial(
                core_kernel, count, 0 if c else head, [0] * half + [tall[0] * c] * half, rows, ranks, views, parts,
                0 if c else groups, len(waits),
            ),
            outs,
            [
                pltpu.VMEM((views, tall[c], width), bf16),
                pltpu.VMEM((width // 128, -(-count // 8) * 8 * ranks, 128), f32),
            ],
            2 * views_all * count * width * ranks,
            whole[c][::-1] + near[::-1] + carried,
            waits,
        )
        lit += swaps(made[:parts], "light")[::-1]
        pieces.append(made[parts])
        carried = list(made[parts + 1 :])
    spans = [(k, 0) for k in range(half)] + [(k, c * tall[0]) for c in range(2) for k in range(half, views)]
    wide = lights_all + views_all // 2
    both = max(lights_all, views_all)
    view_part = call(
        functools.partial(view_kernel, lights, rows, views, spans, view_scale),
        sds((2, both, wide), f32),
        [pltpu.VMEM((views, head + lights * rows, width), bf16)],
        2 * views_all * lights * width * views_all,
        near + whole[0] + whole[1],
    )
    back = call(
        functools.partial(back_kernel, 2), [sds((size * lights, width), bf16)] * views, [], 0, pieces, lit[: parts - 1] + [view_part]
    )
    returned = swaps(back, "view")
    keep, send = call(
        functools.partial(light_kernel, counts, 1, parts, light_scale),
        [sds((both, wide), f32)] * 2,
        [pltpu.VMEM((parts, size * count, width), bf16) for count in counts],
        2 * lights_all * lights_all * size * width,
        lit + [view_part],
        [returned[1]],
    )
    dealt = call(
        functools.partial(deal_light_kernel, lights, parts),
        [sds((views_all // 2, views_all + lights_all // 2), f32)] * parts,
        [pltpu.VMEM((parts, views_all // 2, views_all + lights_all // 2), f32)],
        0,
        [keep, swap(send, "view", 1)],
    )
    total = call(sum_kernel, sds(dealt[0].shape, f32), [], 0, swaps(dealt, "light")[::-1])
    texels, step = lax.axis_size("texel"), 2
    while step < texels:
        total = total + swap(total, "texel", step)
        step *= 2
    dealt = call(
        functools.partial(deal_view_kernel, lights, rows, 2),
        [sds((lights + rows, views_all), f32)] * half,
        [pltpu.VMEM((half, lights + rows, views_all), f32)],
        0,
        [total],
        [returned[2], returned[3]],
    )
    steps = [(t, m) for t in range(min(2, texels) - 1, -1, -1) for m in range(half - 1, -1, -1)]
    came = [swap(dealt[m], ("texel", "view"), t * views + 2 * m) for t, m in steps[:-1]]
    total = summed([dealt[0]] + came[::-1])
    core = call(
        functools.partial(place_kernel, counts),
        sds((ranks // views, lights, columns), bf16),
        [],
        0,
        returned,
    )
    return (total[lights:], core, total[:lights])


def solution(mesh):
    return jax.shard_map(
        body,
        mesh=mesh,
        in_specs=(P("light", "view", "texel"), P("view", None)),
        out_specs=(P("view", None), P("view", "light", "texel"), P("light", None)),
        check_vma=False,
    )
```

```python
import functools

import jax
import jax.numpy as jnp
from jax import lax
from jax.experimental import pallas as pl
from jax.experimental.pallas import tpu as pltpu
from jax.sharding import PartitionSpec as P

VMEM = pl.BlockSpec(memory_space=pltpu.VMEM)
ANY = pl.BlockSpec(memory_space=pl.ANY)
sds = jax.ShapeDtypeStruct
bf16, f32 = jnp.bfloat16, jnp.float32


def swap(value, axis, step):
    return lax.ppermute(value, axis, [(i, i ^ step) for i in range(lax.axis_size(axis))])


def farthest_first(n):
    return list(range(n - 1, -1, -1))


def swaps(values, axis):
    moved = {k: swap(values[k], axis, k) for k in farthest_first(len(values))[:-1]}
    return [values[0]] + [moved[k] for k in range(1, len(values))]


def summed(values):
    total = values[-1]
    for value in values[-2::-1]:
        total = total + value
    return total


def call(kernel, out_shape, scratch, flops, args, unused=()):
    moved = sum(a.size * a.dtype.itemsize for a in list(args) + jax.tree.leaves(out_shape))
    return pl.pallas_call(
        kernel,
        out_shape=out_shape,
        in_specs=[VMEM] * len(args) + [ANY] * len(unused),
        out_specs=jax.tree.map(lambda _: VMEM, out_shape),
        scratch_shapes=scratch,
        compiler_params=pltpu.CompilerParams(vmem_limit_bytes=32 * 1024 * 1024),
        cost_estimate=pl.CostEstimate(flops=flops, bytes_accessed=moved, transcendentals=0),
    )(*args, *unused)


def nt(a, b):
    return lax.dot_general(a, b, (((1,), (1,)), ((), ())), preferred_element_type=f32)


def cut(refs, *counts):
    out, at = [], 0
    for count in counts:
        out.append(refs[at : at + count])
        at += count
    return out + [refs[at:]]


def blank_kernel(out_ref):
    out_ref[...] = jnp.zeros_like(out_ref)


def pack_kernel(spans, groups, ranks, views, slab_ref, *refs):
    me = lax.axis_index("view")
    outs = refs[-len(spans) :]
    rows, columns = slab_ref.shape[1:]
    width = columns // views
    head = []
    if groups:
        deep = rows // groups
        wide = refs[0][...].astype(f32)
        wide = jnp.concatenate([wide[g * deep : (g + 1) * deep] for g in range(groups)], axis=1)
        head = [jnp.pad(wide, ((0, -deep % 16), (0, width - groups * ranks))).astype(bf16)]
    for (k, begin, count), out in zip(spans, outs):
        at = pl.ds(pl.multiple_of((me ^ k) * width, width), width)
        out[...] = jnp.concatenate(head + [slab_ref[l, :, at] for l in range(begin, begin + count)], axis=0)


def core_kernel(lights, head, starts, rows, ranks, views, parts, groups, spare, *refs):
    first = groups > 0
    ins, old, _, light_outs, (pieces, *outs) = cut(refs[:-2], views, 0 if first else 1, spare, parts)
    whole, turned = refs[-2:]
    v, z = lax.axis_index("view"), lax.axis_index("light")
    width = whole.shape[2]
    for i, k in enumerate(farthest_first(views)):
        whole[v ^ k] = ins[i][starts[i] : starts[i] + whole.shape[1], :]
    if first:
        deep = rows // groups
        wide = [whole[k, :head, :].astype(f32)[:deep] for k in range(views)]
        basis = jnp.concatenate([w[:, g * ranks : (g + 1) * ranks] for w in wide for g in range(groups)], axis=0)
        basis = jnp.pad(basis, ((0, 0), (0, 128 - ranks))).T[:ranks].astype(bf16)
    else:
        basis = old[0][...]
    for l in range(lights):
        at = head + l * rows
        page = jnp.concatenate([whole[k, at : at + rows, :] for k in range(views)], axis=0)
        product = jnp.dot(basis, page, preferred_element_type=f32)
        for h in range(width // 128):
            turned[h, l * ranks : (l + 1) * ranks, :] = product[:, h * 128 : (h + 1) * 128]
    size = ranks // parts
    for j in range(parts):
        for h in range(width // 128):
            picked = [turned[h, pl.ds(j * size + r, lights, stride=ranks), :] for r in range(size)]
            pieces[j, :, h * 128 : (h + 1) * 128] = jnp.concatenate(picked, axis=0).astype(bf16)
    for k in range(parts):
        light_outs[k][...] = pieces[z ^ k]
    if first:
        outs[0][...] = basis


def back_kernel(chunks, *refs):
    v, outs = lax.axis_index("view"), refs[-refs[0].shape[0] :]
    for k, out in enumerate(outs):
        out[...] = jnp.concatenate([ref[v ^ k] for ref in refs[:chunks]], axis=0)


def view_kernel(lights, rows, views, spans, scale, *refs):
    ins, (out, whole) = cut(refs, len(spans))
    v = lax.axis_index("view")
    for (k, begin), ref in zip(spans, ins):
        whole[v ^ k, begin : begin + ref.shape[0], :] = ref[...]
    head = whole.shape[1] - lights * rows
    gram = jnp.zeros((views * rows, views * rows), f32)
    for l in range(lights):
        at = head + l * rows
        page = jnp.concatenate([whole[k, at : at + rows, :] for k in range(views)], axis=0)
        gram += nt(page, page)
    gram *= scale
    half = views * rows // 2
    left = jnp.zeros((out.shape[1], out.shape[2] - half), f32)
    for p in range(2):
        mine = jnp.concatenate([gram[k * rows : (k + 1) * rows] for k in range(p, views, 2)], axis=0)
        mine = jnp.concatenate([mine[:, :half], mine[:, half:]], axis=0)
        out[p] = jnp.concatenate([left, mine], axis=1)


def deal_light_kernel(lights, parts, keep_ref, came_ref, *refs):
    outs, blocks = refs[:-1], refs[-1]
    z = lax.axis_index("light")
    total = keep_ref[...] + came_ref[...]
    wide = lights * parts
    tall = total.shape[0] // 2
    view = total[:, total.shape[1] - tall :]
    view = jnp.concatenate([view[:tall], view[tall:]], axis=1)
    for k in range(parts):
        light = total[k * lights : (k + 1) * lights, :wide]
        light = jnp.concatenate([light[:, : wide // 2], light[:, wide // 2 :]], axis=0)
        blocks[k] = jnp.concatenate([view, light], axis=1)
    for k in range(parts):
        outs[k][...] = blocks[z ^ k]


def deal_view_kernel(lights, rows, spare, *refs):
    total_ref, outs, blocks = refs[0], refs[1 + spare : -1], refs[-1]
    u = lax.axis_index("view") // 2
    total = total_ref[...]
    wide = 2 * rows * len(outs)
    light = total[:, wide:]
    light = jnp.concatenate([light[:lights], light[lights:]], axis=1)
    for m in range(len(outs)):
        blocks[m] = jnp.concatenate([light, total[m * rows : (m + 1) * rows, :wide]], axis=0)
    for m in range(len(outs)):
        outs[m][...] = blocks[u ^ m]


def sum_kernel(*refs):
    refs[-1][...] = summed([ref[...] for ref in refs[:-1]])


def light_kernel(counts, spare, parts, scale, *refs):
    ins, (view,), _, (keep_out, send_out), wholes = cut(refs, parts * len(counts), 1, spare, 2)
    z, lights = lax.axis_index("light"), sum(counts)
    for c, whole in enumerate(wholes):
        for i, k in enumerate(farthest_first(parts)):
            whole[z ^ k] = ins[c * parts + i][...]
    gram = jnp.zeros((parts * lights, parts * lights), f32)
    for r in range(wholes[0].shape[1] // counts[0]):
        page = [wholes[c][k, r * n : (r + 1) * n, :] for k in range(parts) for c, n in enumerate(counts)]
        page = jnp.concatenate(page, axis=0)
        gram += nt(page, page)
    gram *= scale
    gram = jnp.pad(gram, ((0, keep_out.shape[0] - gram.shape[0]), (0, keep_out.shape[1] - gram.shape[1])))
    parity = lax.axis_index("view") % 2
    keep_out[...] = gram + view[parity]
    send_out[...] = gram + view[1 - parity]


def place_kernel(counts, *refs):
    ins, core_ref = refs[:-1], refs[-1]
    v = lax.axis_index("view")
    ranks, width = core_ref.shape[0], ins[0].shape[1]
    for k in range(len(ins)):
        at = pl.ds(pl.multiple_of((v ^ k) * width, width), width)
        for r in range(ranks):
            begin, page = 0, []
            for n in counts:
                page.append(ins[k][begin + r * n : begin + (r + 1) * n, :])
                begin += ranks * n
            core_ref[r, :, at] = jnp.concatenate(page, axis=0)


def body(slab, basis):
    views, parts = lax.axis_size("view"), lax.axis_size("light")
    lights, rows, columns = slab.shape
    ranks = basis.shape[1]
    columns_all = columns * lax.axis_size("texel")
    view_scale = 1.0 / (lights * parts * columns_all)
    light_scale = 1.0 / (ranks * columns_all)
    width = columns // views
    views_all, lights_all = views * rows, parts * lights
    size = ranks // parts
    groups = max(g for g in range(1, width // ranks + 1) if rows % g == 0)
    head = -(-(rows // groups) // 16) * 16

    one = lights * 2 // 5 // 4 * 4
    counts, half = [one, lights - one], views // 2
    tall = [head + one * rows, (lights - one) * rows]

    blank = call(blank_kernel, sds((8, 128), f32), [], 10**9, [])

    spans = [(k, 0, lights if k < half else one) for k in range(views)]
    packed = call(
        functools.partial(pack_kernel, spans, groups, ranks, views),
        [sds((head + count * rows, width), bf16) for _, _, count in spans],
        [],
        0,
        [slab, basis],
        [blank],
    )
    came = swaps(packed, "view")
    near, whole = came[:half], [came[half:]]
    spans = [(k, one, lights - one) for k in range(half, views)]
    packed = call(
        functools.partial(pack_kernel, spans, 0, ranks, views),
        [sds((tall[1], width), bf16)] * len(spans),
        [],
        0,
        [slab],
        whole[0][1:],
    )
    moved = {k: swap(packed[k - half], "view", k) for k in farthest_first(views)[:half]}
    whole.append([moved[k] for k in range(half, views)])

    lit, carried, pieces = [], [], []
    for c, count in enumerate(counts):
        outs = [sds((size * count, width), bf16)] * parts + [sds((parts, size * count, width), bf16)]
        if c == 0:
            outs += [sds((ranks, views_all), bf16)]
        waits = lit[:1] if c else []
        made = call(
            functools.partial(
                core_kernel, count, 0 if c else head, [0] * half + [tall[0] * c] * half, rows, ranks, views, parts,
                0 if c else groups, len(waits),
            ),
            outs,
            [
                pltpu.VMEM((views, tall[c], width), bf16),
                pltpu.VMEM((width // 128, -(-count // 8) * 8 * ranks, 128), f32),
            ],
            2 * views_all * count * width * ranks,
            whole[c][::-1] + near[::-1] + carried,
            waits,
        )
        lit += swaps(made[:parts], "light")[::-1]
        pieces.append(made[parts])
        carried = list(made[parts + 1 :])
    back = call(
        functools.partial(back_kernel, 2), [sds((size * lights, width), bf16)] * views, [], 0, pieces, lit[: parts - 1]
    )
    spans = [(k, 0) for k in range(half)] + [(k, c * tall[0]) for c in range(2) for k in range(half, views)]
    wide = lights_all + views_all // 2
    both = max(lights_all, views_all)
    view_part = call(
        functools.partial(view_kernel, lights, rows, views, spans, view_scale),
        sds((2, both, wide), f32),
        [pltpu.VMEM((views, head + lights * rows, width), bf16)],
        2 * views_all * lights * width * views_all,
        near + whole[0] + whole[1],
    )
    returned = swaps(back, "view")
    keep, send = call(
        functools.partial(light_kernel, counts, 1, parts, light_scale),
        [sds((both, wide), f32)] * 2,
        [pltpu.VMEM((parts, size * count, width), bf16) for count in counts],
        2 * lights_all * lights_all * size * width,
        lit + [view_part],
        [returned[1]],
    )
    dealt = call(
        functools.partial(deal_light_kernel, lights, parts),
        [sds((views_all // 2, views_all + lights_all // 2), f32)] * parts,
        [pltpu.VMEM((parts, views_all // 2, views_all + lights_all // 2), f32)],
        0,
        [keep, swap(send, "view", 1)],
    )
    total = call(sum_kernel, sds(dealt[0].shape, f32), [], 0, swaps(dealt, "light")[::-1])
    texels, step = lax.axis_size("texel"), 2
    while step < texels:
        total = total + swap(total, "texel", step)
        step *= 2
    dealt = call(
        functools.partial(deal_view_kernel, lights, rows, 2),
        [sds((lights + rows, views_all), f32)] * half,
        [pltpu.VMEM((half, lights + rows, views_all), f32)],
        0,
        [total],
        [returned[2], returned[3]],
    )
    steps = [(t, m) for t in range(min(2, texels) - 1, -1, -1) for m in range(half - 1, -1, -1)]
    came = [swap(dealt[m], ("texel", "view"), t * views + 2 * m) for t, m in steps[:-1]]
    total = summed([dealt[0], *came[2:], *came[:2]])
    core = call(
        functools.partial(place_kernel, counts),
        sds((ranks // views, lights, columns), bf16),
        [],
        0,
        returned,
    )
    return (total[lights:], core, total[:lights])


def solution(mesh):
    return jax.shard_map(
        body,
        mesh=mesh,
        in_specs=(P("light", "view", "texel"), P("view", None)),
        out_specs=(P("view", None), P("view", "light", "texel"), P("light", None)),
        check_vma=False,
    )
```
